128 devices in a mesh: section: 8 (over y, core), dp: 16 (over z, x).
Axes of the slice: x: 4, y: 4, z: 4, core: 2. Of those that a mesh axis runs over, the one named last changes fastest.
Arguments:
- tokens_in: bfloat16 [2048, 2048], P('dp'), may hold values from -20 to 20
- cotangent: bfloat16 [2048, 2048], P('dp'), may hold values from -6 to 6
- in_weights: bfloat16 [8, 2048, 3072], P('section'), may hold values from -5 to 5, as said below
- out_weights: bfloat16 [8, 1024, 2048], P('section'), may hold values from -0.1875 to 0.1875
- slice_lengths: int32 [16, 8], P('dp'), may hold values from 1 to 32, 128 in all within a row
Outputs:
- section_outputs: bfloat16 [8, 2048, 2048], P('section', 'dp')
- input_grads: bfloat16 [8, 2048, 2048], P('section', 'dp')
- grad_in_weights: bfloat16 [8, 2048, 3072], P('section', 'dp')
- grad_out_weights: bfloat16 [8, 1024, 2048], P('section', None, 'dp')
The draws below stay inside these ranges and needn't reach their ends.
Inputs may be any that keep to these rules, and one draw needn't show every extreme that they name: `slice_lengths`: each row holds the 8 slice lengths of one sequence in order; they sum to 128 and the longest is exactly 32. `in_weights`: projections of queries, keys and values, in that order along the last dimension.
All inputs are finite; a program needn't handle non-finite values.
Results may differ from the reference program's by a relative error of at most 0.034.
Values may be sent and summed in bfloat16 or wider, within the bound.
A program may use at most 192 MiB of HBM per device.

```python
import math
import jax
import jax.numpy as jnp
import numpy as np
from jax import lax

D = 2048
HEADS = 8
HS = 128
HD_ALL = 1024
SEQ = 128
NSLICE = 8
MOST = 32
SECTIONS = 8
SEQS = 16
TOKENS = 2048
N_DP = 16


def draw_tokens_in(key, part):
    key = jax.random.fold_in(key, 11)
    key_base = jax.random.fold_in(key, 0)
    base = jnp.clip(jax.random.normal(key_base, (TOKENS, D), jnp.float32), -6.0, 6.0)
    return base.astype(jnp.bfloat16)


def draw_in_weights(key, part):
    key = jax.random.fold_in(key, 12)
    key_base = jax.random.fold_in(key, 0)
    base = jnp.clip(jax.random.normal(key_base, (SECTIONS, D, 3 * HD_ALL), jnp.float32), -6.0, 6.0) / math.sqrt(D)
    return base.astype(jnp.bfloat16)


def level_of(stream_key, shape, shards, least, largest):
    factor_of, own = 1.0, jax.random.fold_in(stream_key, 6)
    for axis_at, shards_of in shards:
        draws = jnp.exp(jax.random.uniform(jax.random.fold_in(own, axis_at), (shards_of,), jnp.float32, least / len(shards), largest / len(shards)))
        factor_of = factor_of * jnp.repeat(draws, shape[axis_at] // shards_of).reshape([-1 if axis == axis_at else 1 for axis in range(len(shape))])
    return factor_of


def length_profile(amount, total, limit, slope):
    portions = [(1 << 20) // math.isqrt(grade ** slope) + 1 for grade in range(2, amount + 1)]
    surplus, holding = total - limit - (amount - 1), [1] * (amount - 1)
    while surplus > 0:
        movable = [i for i in range(amount - 1) if holding[i] < limit]
        mass, left = sum([portions[i] for i in movable]), surplus
        for i in movable:
            extra = min(limit - holding[i], max(1, left * portions[i] // mass), surplus)
            holding[i] = holding[i] + extra
            surplus = surplus - extra
    return np.array([limit] + holding)


def uneven(stream_key, amount, total, limit, skew):
    if amount == 2:
        one = jax.random.randint(stream_key, (), max(1, total - limit), min(limit, total - 1) + 1)
        return jnp.stack([one, total - one])
    lengths = jnp.asarray(length_profile(amount, total, limit, skew), jnp.int32)
    pairs = (amount - 1) // 2
    giver, taker = lengths[1:1 + 2 * pairs:2], lengths[2:2 + 2 * pairs:2]
    slack = jnp.minimum(giver - 1, limit - taker)
    passed = jax.random.randint(jax.random.fold_in(stream_key, 1), (pairs,), 0, 1 << 20) % (slack + 1)
    lengths = lengths.at[1:1 + 2 * pairs:2].set(giver - passed).at[2:2 + 2 * pairs:2].set(taker + passed)
    return lengths[jax.random.permutation(jax.random.fold_in(stream_key, 2), amount)]


def scatter_about(stream_key, shape, deviation, reach, shards=(), kind=jnp.bfloat16):
    array = jax.random.normal(stream_key, shape, jnp.float32) * deviation
    if len(shards) > 0:
        array = level_of(stream_key, shape, shards, -0.22, 0.18) * array
    return jnp.clip(array, min=-reach, max=reach).astype(kind)


def setup_inputs(seed: int = 0) -> dict:
    key_of = jax.random.split(jax.random.key(seed), 6)
    return {
        "tokens_in": draw_tokens_in(jax.random.fold_in(key_of[5], 71), 0),
        "cotangent": scatter_about(key_of[1], (TOKENS, D), 1.0, 6.0, ((0, 16),)),
        "in_weights": draw_in_weights(jax.random.fold_in(key_of[5], 71), 0),
        "out_weights": scatter_about(key_of[3], (SECTIONS, HD_ALL, D), HD_ALL ** -0.5, 0.1875, ((0, 8),)),
        "slice_lengths": jax.vmap(lambda own: uneven(own, NSLICE, SEQ, MOST, 2))(jax.random.split(key_of[4], SEQS)).reshape((SEQS, NSLICE)).astype(jnp.int32),
    }


def norm_rows(layer_in):
    values = layer_in.astype(jnp.float32)
    centre = lax.optimization_barrier(jnp.mean(values, -1, keepdims=True))
    shifted = values - centre
    inv_std = lax.rsqrt(lax.optimization_barrier(jnp.mean(shifted * shifted, -1, keepdims=True)) + 1e-05)
    return (shifted * inv_std, inv_std)

def forward_section(layer_in, weight_in, weight_out):
    x_hat, inv_std = norm_rows(layer_in)
    normed = x_hat.astype(jnp.bfloat16)
    projected = jnp.dot(normed, weight_in, preferred_element_type=jnp.float32).astype(jnp.bfloat16)
    length = layer_in.shape[0]
    queries = projected[:, :HD_ALL].reshape(length, HEADS, HS).astype(jnp.float32)
    keys_all = projected[:, HD_ALL:2 * HD_ALL].reshape(length, HEADS, HS).astype(jnp.float32)
    values_all = projected[:, 2 * HD_ALL:].reshape(length, HEADS, HS).astype(jnp.float32)
    places = jnp.arange(length, dtype=jnp.int32)
    scores = jnp.einsum('qhd,khd->hqk', queries, keys_all) / math.sqrt(HS)
    scores = jnp.where(places[None, None, :] <= places[None, :, None], scores, -jnp.inf)
    probs = jax.nn.softmax(scores, axis=-1)
    probs_b = probs.astype(jnp.bfloat16)
    mixed = jnp.einsum('hqk,khd->qhd', probs_b.astype(jnp.float32), values_all)
    mixed = mixed.reshape(length, HD_ALL).astype(jnp.bfloat16)
    output = (layer_in.astype(jnp.float32) + jnp.dot(mixed, weight_out, preferred_element_type=jnp.float32)).astype(jnp.bfloat16)
    return (output, (normed, x_hat, inv_std, projected, probs, probs_b, mixed))

def backward_section(upstream, stored, weight_in, weight_out, same_slice):
    normed, x_hat, inv_std, projected, probs, probs_b, mixed = stored
    length = upstream.shape[0]
    queries = projected[:, :HD_ALL].reshape(length, HEADS, HS).astype(jnp.float32)
    keys_all = projected[:, HD_ALL:2 * HD_ALL].reshape(length, HEADS, HS).astype(jnp.float32)
    values_all = projected[:, 2 * HD_ALL:].reshape(length, HEADS, HS).astype(jnp.float32)
    grad_mixed = jnp.dot(upstream, weight_out.T, preferred_element_type=jnp.float32).astype(jnp.bfloat16)
    grad_heads = grad_mixed.reshape(length, HEADS, HS).astype(jnp.float32)
    grad_probs = jnp.einsum('qhd,khd->hqk', grad_heads, values_all)
    row_delta = lax.optimization_barrier(jnp.sum(probs * grad_probs, -1, keepdims=True))
    grad_scores = (probs * (grad_probs - row_delta)).astype(jnp.bfloat16).astype(jnp.float32)
    grad_q = jnp.einsum('hqk,khd->qhd', grad_scores, keys_all) / math.sqrt(HS)
    masked_scores = jnp.where(same_slice[None], grad_scores, 0.0)
    masked_probs = jnp.where(same_slice[None], probs_b.astype(jnp.float32), 0.0)
    grad_k = jnp.einsum('hqk,qhd->khd', masked_scores, queries) / math.sqrt(HS)
    grad_v = jnp.einsum('hqk,qhd->khd', masked_probs, grad_heads)
    grad_proj = jnp.concatenate([grad_q.reshape(length, HD_ALL), grad_k.reshape(length, HD_ALL), grad_v.reshape(length, HD_ALL)], 1).astype(jnp.bfloat16)
    grad_normed = jnp.dot(grad_proj, weight_in.T, preferred_element_type=jnp.float32)
    norm_grad = inv_std * (grad_normed - lax.optimization_barrier(jnp.mean(grad_normed, -1, keepdims=True)) - x_hat * lax.optimization_barrier(jnp.mean(grad_normed * x_hat, -1, keepdims=True)))
    grad_input = (upstream.astype(jnp.float32) + norm_grad).astype(jnp.bfloat16)
    term_in = jnp.dot(normed.T, grad_proj, preferred_element_type=jnp.float32)
    term_out = jnp.dot(mixed.T, upstream, preferred_element_type=jnp.float32)
    return (grad_input, term_in, term_out)

def rounded(term, grad_scale):
    narrow = (term * grad_scale).astype(jnp.bfloat16)
    narrow = lax.optimization_barrier(narrow)
    return narrow.astype(jnp.float32)

def reference(tokens_in, cotangent, in_weights, out_weights, slice_lengths):
    grad_scale = 1.0 / math.sqrt(SEQ * N_DP)

    def one_sequence(carried, item):
        sum_in, sum_out = carried
        seq_tokens, seq_cot, seq_lengths = item
        slice_ends = jnp.cumsum(seq_lengths).astype(jnp.int32)
        places = jnp.arange(SEQ, dtype=jnp.int32)
        slice_of = lax.optimization_barrier(jnp.sum((places[:, None] >= slice_ends[None, :]).astype(jnp.int32), 1))
        same_slice = slice_of[:, None] == slice_of[None, :]
        layer_in = seq_tokens
        section_outs = []
        stored = []
        for layer in range(SECTIONS):
            layer_in, kept = forward_section(layer_in, in_weights[layer], out_weights[layer])
            section_outs.append(layer_in)
            stored.append(kept)
        upstream = seq_cot
        grads = [None] * SECTIONS
        terms_in = [None] * SECTIONS
        terms_out = [None] * SECTIONS
        for layer in reversed(range(SECTIONS)):
            upstream_next, term_in, term_out = backward_section(upstream, stored[layer], in_weights[layer], out_weights[layer], same_slice)
            terms_in[layer] = rounded(term_in, grad_scale)
            terms_out[layer] = rounded(term_out, grad_scale)
            grads[layer] = upstream_next
            upstream = upstream_next
        sum_in = sum_in + jnp.stack(terms_in)
        sum_out = sum_out + jnp.stack(terms_out)
        return ((sum_in, sum_out), (jnp.stack(section_outs), jnp.stack(grads)))
    start_in = jnp.zeros((SECTIONS, D, 3 * HD_ALL), jnp.float32)
    start_out = jnp.zeros((SECTIONS, HD_ALL, D), jnp.float32)
    inputs = (tokens_in.reshape(N_DP, SEQ, D), cotangent.reshape(N_DP, SEQ, D), slice_lengths)
    (sum_in, sum_out), (outs_all, grads_all) = lax.scan(one_sequence, (start_in, start_out), inputs)
    section_outputs = jnp.transpose(outs_all, (1, 0, 2, 3)).reshape(SECTIONS, TOKENS, D)
    input_grads = jnp.transpose(grads_all, (1, 0, 2, 3)).reshape(SECTIONS, TOKENS, D)
    return (section_outputs, input_grads, sum_in.astype(jnp.bfloat16), sum_out.astype(jnp.bfloat16))
```

```python
import math

import jax
import jax.numpy as jnp
from jax import lax
from jax.experimental import pallas as pl
from jax.experimental.pallas import tpu as pltpu
from jax.sharding import PartitionSpec as P

HS = 128
CHUNKS = 1
SUB = 16
MESH = pl.DeviceIdType.MESH
F32 = jnp.float32
BF16 = jnp.bfloat16


def kernel(
    lens,
    tok,
    cot,
    win,
    wout,
    so,
    ig,
    gi,
    go,
    w_in,
    w_out,
    w_in_t,
    w_out_t,
    x_in,
    x_hat,
    inv_std,
    normed,
    proj,
    probs,
    mixed,
    out,
    up,
    grad_mixed,
    key_acc,
    val_acc,
    gp,
    gn,
    gin,
    n_t,
    m_t,
    n_g,
    m_g,
    gp_g,
    up_g,
    part,
    go_buf,
    win_sem,
    wout_sem,
    local_sem,
    own_sem,
    fwd_send,
    fwd_recv,
    bwd_send,
    bwd_recv,
    n_send,
    n_recv,
    m_send,
    m_recv,
    gp_send,
    gp_recv,
    up_send,
    up_recv,
    fin_send,
    fin_recv,
):
    sections = 8
    n_dp = 16
    side = 4
    sec = lax.axis_index("section")
    me = lax.axis_index("dp")
    my_z, my_x = me // side, lax.rem(me, side)
    seq, width = x_in.shape
    inner = w_out.shape[0]
    heads = inner // HS
    rows_c = seq // CHUNKS
    n_rows = width // side
    gp_cols = 3 * inner // side
    up_cols = width // n_dp
    w_blk = win_sem.shape[0]
    w_cols = 3 * inner // w_blk
    scale = 1.0 / math.sqrt(HS)
    grad_scale = 1.0 / math.sqrt(seq * n_dp)

    def win_copy(j):
        cols = pl.ds(j * w_cols, w_cols)
        return pltpu.make_async_copy(win.at[0, :, cols], w_in.at[:, cols], win_sem.at[j])

    wout_copy = pltpu.make_async_copy(wout.at[0], w_out, wout_sem)
    tok_copy = pltpu.make_async_copy(tok, x_in, local_sem.at[0])
    cot_copy = pltpu.make_async_copy(cot, up, local_sem.at[1])

    @pl.when(sec == 0)
    def _():
        tok_copy.start()

    @pl.when(sec == sections - 1)
    def _():
        cot_copy.start()

    for j in range(w_blk):
        win_copy(j).start()
    wout_copy.start()

    barrier = pltpu.get_barrier_semaphore()

    def greet(d, _):
        pl.semaphore_signal(
            barrier, inc=1, device_id={"dp": lax.rem(me + d, n_dp)}, device_id_type=MESH
        )
        return 0

    lax.fori_loop(1, n_dp, greet, 0)
    for step in (1, sections - 1):
        pl.semaphore_signal(
            barrier,
            inc=1,
            device_id={"section": lax.rem(sec + step, sections)},
            device_id_type=MESH,
        )
    pl.semaphore_wait(barrier, n_dp + 1)

    row_at = lax.broadcasted_iota(jnp.int32, (seq, seq), 0)
    col_at = lax.broadcasted_iota(jnp.int32, (seq, seq), 1)
    row_slice = jnp.zeros((seq, seq), jnp.int32)
    col_slice = jnp.zeros((seq, seq), jnp.int32)
    end = jnp.int32(0)
    for j in range(lens.shape[1]):
        end = end + lens[0, j]
        row_slice = row_slice + jnp.where(row_at >= end, 1, 0)
        col_slice = col_slice + jnp.where(col_at >= end, 1, 0)
    same = row_slice == col_slice
    causal = col_at <= row_at
    if CHUNKS > 1:
        proj[...] = jnp.zeros_like(proj)

    def transpose_weights():
        blk = 512

        def turn(source, dest):
            rows, cols = source.shape
            wide = cols // blk

            def one(i, _):
                r = pl.multiple_of((i // wide) * blk, blk)
                c = pl.multiple_of(lax.rem(i, wide) * blk, blk)
                dest[pl.ds(c, blk), pl.ds(r, blk)] = source[pl.ds(r, blk), pl.ds(c, blk)].T
                return 0

            lax.fori_loop(0, (rows // blk) * wide, one, 0)

        turn(w_in, w_in_t)
        turn(w_out, w_out_t)

    @pl.when(sec > 0)
    def _():
        for j in range(w_blk):
            win_copy(j).wait()
        wout_copy.wait()

    @pl.when(sec >= sections // 2)
    def _():
        transpose_weights()

    def fwd_hop(c):
        rows = pl.ds(c * rows_c, rows_c)
        return pltpu.make_async_remote_copy(
            src_ref=out.at[rows],
            dst_ref=x_in.at[rows],
            send_sem=fwd_send.at[c],
            recv_sem=fwd_recv.at[c],
            device_id={"section": lax.rem(sec + 1, sections)},
            device_id_type=MESH,
        )

    def so_copy(c):
        rows = pl.ds(c * rows_c, rows_c)
        return pltpu.make_async_copy(out.at[rows], so.at[0, rows], local_sem.at[2 + c])

    @pl.when(sec == 0)
    def _():
        tok_copy.wait()

    for c in range(CHUNKS):
        r0 = c * rows_c
        rows = slice(r0, r0 + rows_c)

        @pl.when(sec > 0)
        def _():
            fwd_hop(c).wait_recv()

        for r in range(r0, r0 + rows_c, SUB):
            sub = slice(r, r + SUB)
            values = x_in[sub, :].astype(F32)
            centre = jnp.mean(values, -1, keepdims=True)
            shifted = values - centre
            inv = lax.rsqrt(jnp.mean(shifted * shifted, -1, keepdims=True) + 1e-05)
            hat = shifted * inv
            x_hat[sub, :] = hat
            inv_std[sub, :] = jnp.broadcast_to(inv, (SUB, 128))
            normed[sub, :] = hat.astype(BF16)

        for j in range(w_blk):
            if c == 0:

                @pl.when(sec == 0)
                def _():
                    win_copy(j).wait()

            cols = slice(j * w_cols, (j + 1) * w_cols)
            proj[rows, cols] = jnp.dot(
                normed[rows, :], w_in[:, cols], preferred_element_type=F32
            ).astype(BF16)

        for h in range(heads):
            q = proj[rows, h * HS : (h + 1) * HS]
            k = proj[:, inner + h * HS : inner + (h + 1) * HS]
            v = proj[:, 2 * inner + h * HS : 2 * inner + (h + 1) * HS]
            scores = (
                lax.dot_general(q, k, (((1,), (1,)), ((), ())), preferred_element_type=F32) * scale
            )
            scores = jnp.where(causal[rows, :], scores, -jnp.inf)
            top = jnp.max(scores, -1, keepdims=True)
            weight = jnp.exp(scores - top)
            p = weight / jnp.sum(weight, -1, keepdims=True)
            probs[h, rows, :] = p
            mixed[rows, h * HS : (h + 1) * HS] = jnp.dot(
                p.astype(BF16), v, preferred_element_type=F32
            ).astype(BF16)

        if c == 0:

            @pl.when(sec == 0)
            def _():
                wout_copy.wait()

        for j in range(0, width, 512):
            cols = slice(j, j + 512)
            out[rows, cols] = (
                x_in[rows, cols].astype(F32)
                + jnp.dot(mixed[rows, :], w_out[:, cols], preferred_element_type=F32)
            ).astype(BF16)

        @pl.when(sec < sections - 1)
        def _():
            fwd_hop(c).start()

        so_copy(c).start()

    def partner(d):
        to = lax.rem(me + d, n_dp)
        return to, to // side, lax.rem(to, side)

    mine = pl.ds(pl.multiple_of(me * seq, seq), seq)

    def n_copy(d):
        to, z, _ = partner(d)
        return pltpu.make_async_remote_copy(
            src_ref=n_t.at[pl.ds(pl.multiple_of(z * n_rows, n_rows), n_rows)],
            dst_ref=n_g.at[:, mine],
            send_sem=n_send.at[d],
            recv_sem=n_recv.at[d],
            device_id={"dp": to},
            device_id_type=MESH,
        )

    def m_copy(d):
        to, _, _ = partner(d)
        return pltpu.make_async_remote_copy(
            src_ref=m_t,
            dst_ref=m_g.at[:, mine],
            send_sem=m_send.at[d],
            recv_sem=m_recv.at[d],
            device_id={"dp": to},
            device_id_type=MESH,
        )

    def up_copy(d):
        to, _, _ = partner(d)
        return pltpu.make_async_remote_copy(
            src_ref=up.at[:, pl.ds(pl.multiple_of(to * up_cols, up_cols), up_cols)],
            dst_ref=up_g.at[mine],
            send_sem=up_send.at[d],
            recv_sem=up_recv.at[d],
            device_id={"dp": to},
            device_id_type=MESH,
        )

    def gp_copy(c, d):
        to, _, x = partner(d)
        return pltpu.make_async_remote_copy(
            src_ref=gp.at[
                pl.ds(c * rows_c, rows_c), pl.ds(pl.multiple_of(x * gp_cols, gp_cols), gp_cols)
            ],
            dst_ref=gp_g.at[pl.ds(pl.multiple_of(me * seq + c * rows_c, rows_c), rows_c)],
            send_sem=gp_send.at[c, d],
            recv_sem=gp_recv.at[c, d],
            device_id={"dp": to},
            device_id_type=MESH,
        )

    n_own = pltpu.make_async_copy(
        n_t.at[pl.ds(pl.multiple_of(my_z * n_rows, n_rows), n_rows)], n_g.at[:, mine], own_sem.at[0]
    )
    m_own = pltpu.make_async_copy(m_t, m_g.at[:, mine], own_sem.at[1])
    up_own = pltpu.make_async_copy(
        up.at[:, pl.ds(pl.multiple_of(me * up_cols, up_cols), up_cols)],
        up_g.at[mine],
        own_sem.at[2],
    )
    gp_own = pltpu.make_async_copy(
        gp.at[:, pl.ds(pl.multiple_of(my_x * gp_cols, gp_cols), gp_cols)],
        gp_g.at[mine],
        own_sem.at[3],
    )

    def each(start, *fns):
        def one(d, _):
            for fn in fns:
                fn(d)
            return 0

        lax.fori_loop(1, n_dp, one, 0)

    for r in range(0, width, 512):
        n_t[r : r + 512, :] = normed[:, r : r + 512].T
    for r in range(0, inner, 512):
        m_t[r : r + 512, :] = mixed[:, r : r + 512].T
    each(None, lambda d: n_copy(d).start(), lambda d: m_copy(d).start())
    n_own.start()
    m_own.start()

    @pl.when(sec < sections // 2)
    def _():
        transpose_weights()

    def bwd_hop(c):
        rows = pl.ds(c * rows_c, rows_c)
        return pltpu.make_async_remote_copy(
            src_ref=gin.at[rows],
            dst_ref=up.at[rows],
            send_sem=bwd_send.at[c],
            recv_sem=bwd_recv.at[c],
            device_id={"section": lax.rem(sec + sections - 1, sections)},
            device_id_type=MESH,
        )

    def ig_copy(c):
        rows = pl.ds(c * rows_c, rows_c)
        return pltpu.make_async_copy(gin.at[rows], ig.at[0, rows], local_sem.at[2 + CHUNKS + c])

    @pl.when(sec == sections - 1)
    def _():
        cot_copy.wait()

    for c in reversed(range(CHUNKS)):
        r0 = c * rows_c
        rows = slice(r0, r0 + rows_c)

        @pl.when(sec < sections - 1)
        def _():
            bwd_hop(c).wait_recv()

        for j in range(0, inner, 512):
            cols = slice(j, j + 512)
            grad_mixed[rows, cols] = jnp.dot(
                up[rows, :], w_out_t[:, cols], preferred_element_type=F32
            ).astype(BF16)

        for h in range(heads):
            at = slice(h * HS, (h + 1) * HS)
            k_at = slice(inner + h * HS, inner + (h + 1) * HS)
            v_at = slice(2 * inner + h * HS, 2 * inner + (h + 1) * HS)
            q, k, v = proj[rows, at], proj[:, k_at], proj[:, v_at]
            g = grad_mixed[rows, at]
            p = probs[h, rows, :]
            grad_p = lax.dot_general(g, v, (((1,), (1,)), ((), ())), preferred_element_type=F32)
            delta = jnp.sum(p * grad_p, -1, keepdims=True)
            grad_s = p * (grad_p - delta)
            gp[rows, at] = (
                jnp.dot(grad_s.astype(BF16), k, preferred_element_type=F32) * scale
            ).astype(BF16)
            live = same[rows, :]
            grad_s = jnp.where(live, grad_s, 0.0).astype(BF16)
            p = jnp.where(live, p, 0.0).astype(BF16)
            gk = lax.dot_general(grad_s, q, (((0,), (0,)), ((), ())), preferred_element_type=F32)
            gv = lax.dot_general(p, g, (((0,), (0,)), ((), ())), preferred_element_type=F32)
            if c < CHUNKS - 1:
                gk = gk + key_acc[:, at]
                gv = gv + val_acc[:, at]
            if c > 0:
                key_acc[:, at] = gk
                val_acc[:, at] = gv
            gp[rows, k_at] = (gk[rows, :] * scale).astype(BF16)
            gp[rows, v_at] = gv[rows, :].astype(BF16)

        @pl.when(sec == 0)
        def _():
            each(None, lambda d: gp_copy(c, d).start())

        for j in range(0, width, 512):
            cols = slice(j, j + 512)
            gn[rows, cols] = jnp.dot(gp[rows, :], w_in_t[:, cols], preferred_element_type=F32)

        for r in range(r0, r0 + rows_c, SUB):
            sub = slice(r, r + SUB)
            g = gn[sub, :]
            hat = x_hat[sub, :]
            mean_g = jnp.mean(g, -1, keepdims=True)
            mean_gh = jnp.mean(g * hat, -1, keepdims=True)
            grad = inv_std[sub, :1] * (g - mean_g - hat * mean_gh)
            gin[sub, :] = (up[sub, :].astype(F32) + grad).astype(BF16)

        @pl.when(sec > 0)
        def _():
            bwd_hop(c).start()
            each(None, lambda d: gp_copy(c, d).start())

        ig_copy(c).start()

    each(None, lambda d: up_copy(d).start())
    up_own.start()
    gp_own.start()

    m_own.wait()
    up_own.wait()
    each(None, lambda d: m_copy(d).wait_recv(), lambda d: up_copy(d).wait_recv())
    for r in range(0, inner, 256):
        go_buf[r : r + 256, :] = (
            jnp.dot(m_g[r : r + 256, :], up_g[...], preferred_element_type=F32) * grad_scale
        ).astype(BF16)
    go_copy = pltpu.make_async_copy(go_buf, go.at[0], local_sem.at[2 + 2 * CHUNKS])
    go_copy.start()

    n_own.wait()
    gp_own.wait()
    each(
        None,
        lambda d: n_copy(d).wait_recv(),
        *[lambda d, c=c: gp_copy(c, d).wait_recv() for c in range(CHUNKS)],
    )

    def fin_copy(d):
        x = lax.rem(my_x + d, side)
        return pltpu.make_async_remote_copy(
            src_ref=part.at[d],
            dst_ref=gi.at[0, :, pl.ds(pl.multiple_of(my_x * gp_cols, gp_cols), gp_cols)],
            send_sem=fin_send.at[d],
            recv_sem=fin_recv.at[d],
            device_id={"dp": my_z * side + x},
            device_id_type=MESH,
        )

    fin_own = pltpu.make_async_copy(
        part.at[0],
        gi.at[0, :, pl.ds(pl.multiple_of(my_x * gp_cols, gp_cols), gp_cols)],
        own_sem.at[4],
    )
    for d in (2, 1, 3, 0):
        x = lax.rem(my_x + d, side)
        part[d] = (
            jnp.dot(
                n_g[pl.ds(pl.multiple_of(x * seq, seq), seq), :],
                gp_g[...],
                preferred_element_type=F32,
            )
            * grad_scale
        ).astype(BF16)
        if d:
            fin_copy(d).start()
        else:
            fin_own.start()

    each(
        None,
        lambda d: n_copy(d).wait_send(),
        lambda d: m_copy(d).wait_send(),
        lambda d: up_copy(d).wait_send(),
        *[lambda d, c=c: gp_copy(c, d).wait_send() for c in range(CHUNKS)],
    )
    for c in range(CHUNKS):

        @pl.when(sec < sections - 1)
        def _():
            fwd_hop(c).wait_send()

        @pl.when(sec > 0)
        def _():
            bwd_hop(c).wait_send()

        so_copy(c).wait()
        ig_copy(c).wait()
    go_copy.wait()
    fin_own.wait()
    for d in (1, 2, 3):
        fin_copy(d).wait()


def on_device(tokens_in, cotangent, in_weights, out_weights, slice_lengths):
    seq, width = tokens_in.shape
    inner = out_weights.shape[1]
    heads = inner // HS
    n_dp, side = 16, 4
    any_space = pl.BlockSpec(memory_space=pl.ANY)
    vmem = pltpu.VMEM
    dma = pltpu.SemaphoreType.DMA
    w_blk = 4
    scratch = [
        vmem((width, 3 * inner), BF16),
        vmem((inner, width), BF16),
        vmem((3 * inner, width), BF16),
        vmem((width, inner), BF16),
        vmem((seq, width), BF16),
        vmem((seq, width), F32),
        vmem((seq, 128), F32),
        vmem((seq, width), BF16),
        vmem((seq, 3 * inner), BF16),
        vmem((heads, seq, seq), F32),
        vmem((seq, inner), BF16),
        vmem((seq, width), BF16),
        vmem((seq, width), BF16),
        vmem((seq, inner), BF16),
        vmem((seq, inner), F32),
        vmem((seq, inner), F32),
        vmem((seq, 3 * inner), BF16),
        vmem((seq, width), F32),
        vmem((seq, width), BF16),
        vmem((width, seq), BF16),
        vmem((inner, seq), BF16),
        vmem((width // side, n_dp * seq), BF16),
        vmem((inner, n_dp * seq), BF16),
        vmem((n_dp * seq, 3 * inner // side), BF16),
        vmem((n_dp * seq, width // n_dp), BF16),
        vmem((side, seq, 3 * inner // side), BF16),
        vmem((inner, width // n_dp), BF16),
        dma((w_blk,)),
        dma,
        dma((3 + 2 * CHUNKS,)),
        dma((5,)),
        dma((CHUNKS,)),
        dma((CHUNKS,)),
        dma((CHUNKS,)),
        dma((CHUNKS,)),
        dma((n_dp,)),
        dma((n_dp,)),
        dma((n_dp,)),
        dma((n_dp,)),
        dma((CHUNKS, n_dp)),
        dma((CHUNKS, n_dp)),
        dma((n_dp,)),
        dma((n_dp,)),
        dma((side,)),
        dma((side,)),
    ]
    return pl.pallas_call(
        kernel,
        out_shape=(
            jax.ShapeDtypeStruct((1, seq, width), BF16),
            jax.ShapeDtypeStruct((1, seq, width), BF16),
            jax.ShapeDtypeStruct((1, width // n_dp, 3 * inner), BF16),
            jax.ShapeDtypeStruct((1, inner, width // n_dp), BF16),
        ),
        in_specs=[pl.BlockSpec(memory_space=pltpu.SMEM)] + [any_space] * 4,
        out_specs=[any_space] * 4,
        scratch_shapes=scratch,
        compiler_params=pltpu.CompilerParams(
            collective_id=0, has_side_effects=True, vmem_limit_bytes=60 << 20
        ),
    )(slice_lengths, tokens_in, cotangent, in_weights, out_weights)


def solution(mesh):
    placed = (
        P("dp", None),
        P("dp", None),
        P("section", None, None),
        P("section", None, None),
        P("dp", None),
    )
    return jax.shard_map(
        on_device,
        mesh=mesh,
        in_specs=placed,
        out_specs=(
            P("section", "dp", None),
            P("section", "dp", None),
            P("section", "dp", None),
            P("section", None, "dp"),
        ),
        check_vma=False,
    )
```

```python
import math

import jax
import jax.numpy as jnp
from jax import lax
from jax.experimental import pallas as pl
from jax.experimental.pallas import tpu as pltpu
from jax.sharding import PartitionSpec as P

HS = 128
CHUNKS = 2
PIECES = 4
PARTS = 2
SUB = 16
MESH = pl.DeviceIdType.MESH
F32 = jnp.float32
BF16 = jnp.bfloat16


def padded(rows):
    missing = 128 - rows.shape[0]
    if missing <= 0:
        return rows
    return jnp.concatenate([rows, jnp.zeros((missing, rows.shape[1]), rows.dtype)], 0)


def product(rows, weight):
    return jnp.dot(padded(rows), weight, preferred_element_type=F32)[: rows.shape[0]]


def against_rows(left, right):
    return lax.dot_general(left, right, (((1,), (1,)), ((), ())), preferred_element_type=F32)


def over_rows(left, right):
    return lax.dot_general(left, right, (((0,), (0,)), ((), ())), preferred_element_type=F32)


def kernel(
    lens,
    tok,
    cot,
    win,
    wout,
    so,
    ig,
    gi,
    go,
    w_in,
    w_out,
    w_in_t,
    w_out_t,
    x_in,
    x_hat,
    inv_std,
    normed,
    proj,
    probs,
    mixed,
    out,
    up,
    grad_mixed,
    key_acc,
    val_acc,
    gp,
    gn,
    gin,
    n_t,
    m_t,
    up4,
    n_x,
    n_z,
    m_x,
    m_z,
    gp_x,
    gp_z,
    up_x,
    up_z,
    p_x,
    p_z,
    o_x,
    o_z,
    r_x,
    r_z,
    s_x,
    s_z,
    ro_x,
    ro_z,
    go_buf,
    win_sem,
    wout_sem,
    local_sem,
    own_sem,
    fwd_send,
    fwd_recv,
    bwd_send,
    bwd_recv,
    dp_send,
    dp_recv,
):
    sections = 8
    n_dp = 16
    side = 4
    sec = lax.axis_index("section")
    me = lax.axis_index("dp")
    my_z, my_x = me // side, lax.rem(me, side)
    seq, width = x_in.shape
    inner = w_out.shape[0]
    heads = inner // HS
    rows_c = seq // CHUNKS
    quarter = width // side
    half_cols = 3 * inner // 2
    gp_cols = half_cols // side
    half_in = inner // 2
    w_blk = win_sem.shape[0]
    w_cols = 3 * inner // w_blk
    scale = 1.0 / math.sqrt(HS)
    grad_scale = 1.0 / math.sqrt(seq * n_dp)
    piece_cols = width // PIECES

    def aligned(index, size):
        return pl.ds(pl.multiple_of(index * size, size), size)

    def win_copy(j):
        cols = pl.ds(j * w_cols, w_cols)
        return pltpu.make_async_copy(win.at[0, :, cols], w_in.at[:, cols], win_sem.at[j])

    wout_copy = pltpu.make_async_copy(wout.at[0], w_out, wout_sem)
    tok_copy = pltpu.make_async_copy(tok, x_in, local_sem.at[0])
    cot_copy = pltpu.make_async_copy(cot, up, local_sem.at[1])

    @pl.when(sec == 0)
    def _():
        tok_copy.start()

    @pl.when(sec == sections - 1)
    def _():
        cot_copy.start()

    for j in range(w_blk):
        win_copy(j).start()
    wout_copy.start()

    def at_x(d):
        return my_z * side + lax.rem(my_x + d, side)

    def at_z(d):
        return lax.rem(my_z + d, side) * side + my_x

    barrier = pltpu.get_barrier_semaphore()
    for d in (1, 2, 3):
        for to in (at_x(d), at_z(d)):
            pl.semaphore_signal(barrier, inc=1, device_id={"dp": to}, device_id_type=MESH)
    for step in (1, sections - 1):
        pl.semaphore_signal(
            barrier,
            inc=1,
            device_id={"section": lax.rem(sec + step, sections)},
            device_id_type=MESH,
        )

    row_at = lax.broadcasted_iota(jnp.int32, (seq, seq), 0)
    col_at = lax.broadcasted_iota(jnp.int32, (seq, seq), 1)
    causal = col_at <= row_at
    if CHUNKS > 1:
        proj[...] = jnp.zeros_like(proj)
    pl.semaphore_wait(barrier, 8)

    def transpose_weights():
        blk = 512

        def turn(source, dest):
            rows, cols = source.shape
            wide = cols // blk

            def one(i, _):
                r = pl.multiple_of((i // wide) * blk, blk)
                c = pl.multiple_of(lax.rem(i, wide) * blk, blk)
                dest[pl.ds(c, blk), pl.ds(r, blk)] = source[pl.ds(r, blk), pl.ds(c, blk)].T
                return 0

            lax.fori_loop(0, (rows // blk) * wide, one, 0)

        turn(w_in, w_in_t)
        turn(w_out, w_out_t)

    @pl.when(sec > 0)
    def _():
        for j in range(w_blk):
            win_copy(j).wait()
        wout_copy.wait()

    @pl.when(sec >= sections // 2)
    def _():
        transpose_weights()

    def fwd_hop(c, j):
        at = (pl.ds(c * rows_c, rows_c), pl.ds(j * piece_cols, piece_cols))
        return pltpu.make_async_remote_copy(
            src_ref=out.at[at],
            dst_ref=x_in.at[at],
            send_sem=fwd_send.at[c, j],
            recv_sem=fwd_recv.at[c, j],
            device_id={"section": lax.rem(sec + 1, sections)},
            device_id_type=MESH,
        )

    def so_copy(c):
        rows = pl.ds(c * rows_c, rows_c)
        return pltpu.make_async_copy(out.at[rows], so.at[0, rows], local_sem.at[2 + c])

    @pl.when(sec == 0)
    def _():
        tok_copy.wait()

    every = range(heads)
    q_at = [slice(h * HS, (h + 1) * HS) for h in every]
    k_at = [slice(inner + h * HS, inner + (h + 1) * HS) for h in every]
    v_at = [slice(2 * inner + h * HS, 2 * inner + (h + 1) * HS) for h in every]

    for c in range(CHUNKS):
        r0 = c * rows_c
        rows = slice(r0, r0 + rows_c)

        @pl.when(sec > 0)
        def _():
            for j in range(PIECES):
                fwd_hop(c, j).wait_recv()

        for r in range(r0, r0 + rows_c, SUB):
            sub = slice(r, r + SUB)
            values = x_in[sub, :].astype(F32)
            centre = jnp.mean(values, -1, keepdims=True)
            shifted = values - centre
            inv = lax.rsqrt(jnp.mean(shifted * shifted, -1, keepdims=True) + 1e-05)
            hat = shifted * inv
            x_hat[sub, :] = hat
            inv_std[sub, :] = jnp.broadcast_to(inv, (SUB, 128))
            normed[sub, :] = hat.astype(BF16)

        for j in range(w_blk):
            if c == 0:

                @pl.when(sec == 0)
                def _():
                    win_copy(j).wait()

            cols = slice(j * w_cols, (j + 1) * w_cols)
            proj[rows, cols] = product(normed[rows, :], w_in[:, cols]).astype(BF16)

        seen = causal[rows, :]
        scores = [against_rows(proj[rows, q_at[h]], proj[:, k_at[h]]) for h in every]
        scores = [jnp.where(seen, a, -jnp.inf) for a in scores]
        top = [jnp.max(a, -1, keepdims=True) for a in scores]
        weight = [jnp.exp((a - t) * scale) for a, t in zip(scores, top)]
        total = [1.0 / jnp.sum(a, -1, keepdims=True) for a in weight]
        p = [a * t for a, t in zip(weight, total)]
        for h in every:
            probs[h, rows, :] = p[h]
        mixes = [
            jnp.dot(p[h].astype(BF16), proj[:, v_at[h]], preferred_element_type=F32) for h in every
        ]
        for h in every:
            mixed[rows, q_at[h]] = mixes[h].astype(BF16)

        if c == 0:

            @pl.when(sec == 0)
            def _():
                wout_copy.wait()

        for j in range(PIECES):
            cols = slice(j * piece_cols, (j + 1) * piece_cols)
            out[rows, cols] = (
                x_in[rows, cols].astype(F32) + product(mixed[rows, :], w_out[:, cols])
            ).astype(BF16)

            @pl.when(sec < sections - 1)
            def _():
                fwd_hop(c, j).start()

        so_copy(c).start()

    n_kind, m_kind, up_kind, r_kind, ro_kind, fin_kind, gp_kind = range(7)
    mine_x, mine_z = aligned(my_x, seq), aligned(my_z, seq)

    def dp_copy(src, dst, kind, axis, d):
        return pltpu.make_async_remote_copy(
            src_ref=src,
            dst_ref=dst,
            send_sem=dp_send.at[kind, axis, d],
            recv_sem=dp_recv.at[kind, axis, d],
            device_id={"dp": at_z(d) if axis else at_x(d)},
            device_id_type=MESH,
        )

    def n_copies(d):
        return (
            dp_copy(n_t, n_x.at[:, mine_x], n_kind, 0, d),
            dp_copy(n_t, n_z.at[:, mine_z], n_kind, 1, d),
        )

    def m_copies(d):
        return (
            dp_copy(m_t.at[:half_in], m_x.at[:, mine_x], m_kind, 0, d),
            dp_copy(m_t.at[half_in:], m_z.at[:, mine_z], m_kind, 1, d),
        )

    def up_copies(d):
        x, z = lax.rem(my_x + d, side), lax.rem(my_z + d, side)
        return (
            dp_copy(up4.at[:, x], up_x.at[:, mine_x], up_kind, 0, d),
            dp_copy(up4.at[z], up_z.at[:, mine_z], up_kind, 1, d),
        )

    def gp_copies(c, d):
        x, z = lax.rem(my_x + d, side), lax.rem(my_z + d, side)
        rows = pl.ds(c * rows_c, rows_c)
        z_cols = pl.ds(pl.multiple_of(half_cols + z * gp_cols, gp_cols), gp_cols)
        return (
            dp_copy(
                gp.at[rows, aligned(x, gp_cols)],
                gp_x.at[my_x, rows],
                gp_kind + c,
                0,
                d,
            ),
            dp_copy(gp.at[rows, z_cols], gp_z.at[my_z, rows], gp_kind + c, 1, d),
        )

    def r_copies(d):
        x, z = lax.rem(my_x + d, side), lax.rem(my_z + d, side)
        return (
            dp_copy(p_z.at[x], r_z.at[d], r_kind, 0, d),
            dp_copy(p_x.at[z], r_x.at[d], r_kind, 1, d),
        )

    def ro_copies(d):
        x, z = lax.rem(my_x + d, side), lax.rem(my_z + d, side)
        return (
            dp_copy(o_z.at[x], ro_z.at[d], ro_kind, 0, d),
            dp_copy(o_x.at[z], ro_x.at[d], ro_kind, 1, d),
        )

    fin_x = gi.at[0, :, aligned(my_x, gp_cols)]
    fin_z = gi.at[0, :, pl.ds(pl.multiple_of(half_cols + my_z * gp_cols, gp_cols), gp_cols)]

    def fin_copies(d):
        x, z = lax.rem(my_x + d, side), lax.rem(my_z + d, side)
        return (
            dp_copy(s_x.at[x], fin_x, fin_kind, 0, d),
            dp_copy(s_z.at[z], fin_z, fin_kind, 1, d),
        )

    def start(*pairs):
        for pair in pairs:
            for copy in pair:
                copy.start()

    def arrived(copies):
        for d in (1, 3, 2):
            for copy in copies(d):
                copy.wait_recv()

    def send_forward_operands():
        for r in range(0, width, 512):
            n_t[r : r + 512, :] = normed[:, r : r + 512].T
        for r in range(0, inner, 512):
            m_t[r : r + 512, :] = mixed[:, r : r + 512].T
        for d in (2, 1, 3):
            start(n_copies(d), m_copies(d))

    @pl.when(sec < sections - 1)
    def _():
        send_forward_operands()

    @pl.when(sec < sections // 2)
    def _():
        transpose_weights()

    row_slice = jnp.zeros((seq, seq), jnp.int32)
    col_slice = jnp.zeros((seq, seq), jnp.int32)
    end = jnp.int32(0)
    for j in range(lens.shape[1]):
        end = end + lens[0, j]
        row_slice = row_slice + jnp.where(row_at >= end, 1, 0)
        col_slice = col_slice + jnp.where(col_at >= end, 1, 0)
    same = row_slice == col_slice

    def bwd_hop(c):
        rows = pl.ds(c * rows_c, rows_c)
        return pltpu.make_async_remote_copy(
            src_ref=gin.at[rows],
            dst_ref=up.at[rows],
            send_sem=bwd_send.at[c],
            recv_sem=bwd_recv.at[c],
            device_id={"section": lax.rem(sec + sections - 1, sections)},
            device_id_type=MESH,
        )

    def ig_copy(c):
        rows = pl.ds(c * rows_c, rows_c)
        return pltpu.make_async_copy(gin.at[rows], ig.at[0, rows], local_sem.at[2 + CHUNKS + c])

    @pl.when(sec == sections - 1)
    def _():
        cot_copy.wait()

    for c in reversed(range(CHUNKS)):
        r0 = c * rows_c
        rows = slice(r0, r0 + rows_c)

        @pl.when(sec < sections - 1)
        def _():
            bwd_hop(c).wait_recv()

        for j in range(0, inner, 512):
            cols = slice(j, j + 512)
            grad_mixed[rows, cols] = product(up[rows, :], w_out_t[:, cols]).astype(BF16)

        live = same[rows, :]
        grad_p = [against_rows(grad_mixed[rows, q_at[h]], proj[:, v_at[h]]) for h in every]
        p = [probs[h, rows, :] for h in every]
        own_p = [jnp.where(live, a, 0.0).astype(BF16) for a in p]
        grad_v = [over_rows(own_p[h], grad_mixed[rows, q_at[h]]) for h in every]
        weighted = [a * b for a, b in zip(p, grad_p)]
        delta = [jnp.sum(a, -1, keepdims=True) for a in weighted]
        grad_s = [a * (b - t) for a, b, t in zip(p, grad_p, delta)]
        grad_q = [
            jnp.dot(grad_s[h].astype(BF16), proj[:, k_at[h]], preferred_element_type=F32)
            for h in every
        ]
        own_s = [jnp.where(live, a, 0.0).astype(BF16) for a in grad_s]
        grad_k = [over_rows(own_s[h], proj[rows, q_at[h]]) for h in every]
        for h in every:
            gk, gv = grad_k[h], grad_v[h]
            if c < CHUNKS - 1:
                gk = gk[: r0 + rows_c] + key_acc[: r0 + rows_c, q_at[h]]
                gv = gv[: r0 + rows_c] + val_acc[: r0 + rows_c, q_at[h]]
            if c > 0:
                key_acc[:r0, q_at[h]] = gk[:r0]
                val_acc[:r0, q_at[h]] = gv[:r0]
            gp[rows, q_at[h]] = (grad_q[h] * scale).astype(BF16)
            gp[rows, k_at[h]] = (gk[rows] * scale).astype(BF16)
            gp[rows, v_at[h]] = gv[rows].astype(BF16)

        @pl.when(sec == 0)
        def _():
            for d in (2, 1, 3):
                start(gp_copies(c, d))

        for j in range(0, width, 512):
            cols = slice(j, j + 512)
            gn[rows, cols] = product(gp[rows, :], w_in_t[:, cols])

        for r in range(r0, r0 + rows_c, SUB):
            sub = slice(r, r + SUB)
            g = gn[sub, :]
            hat = x_hat[sub, :]
            mean_g = jnp.mean(g, -1, keepdims=True)
            mean_gh = jnp.mean(g * hat, -1, keepdims=True)
            grad = inv_std[sub, :1] * (g - mean_g - hat * mean_gh)
            gin[sub, :] = (up[sub, :].astype(F32) + grad).astype(BF16)

        @pl.when(sec > 0)
        def _():
            bwd_hop(c).start()
            for d in (2, 1, 3):
                start(gp_copies(c, d))

        ig_copy(c).start()

    for b in range(n_dp):
        up4[b // side, b % side] = up[:, b * seq : (b + 1) * seq]
    for d in (2, 1, 3):
        start(up_copies(d))

    @pl.when(sec == sections - 1)
    def _():
        send_forward_operands()

    n_x[:, mine_x] = n_t[...]
    n_z[:, mine_z] = n_t[...]
    m_x[:, mine_x] = m_t[:half_in]
    m_z[:, mine_z] = m_t[half_in:]
    gp_x[my_x] = gp[:, aligned(my_x, gp_cols)]
    gp_z[my_z] = gp[:, pl.ds(pl.multiple_of(half_cols + my_z * gp_cols, gp_cols), gp_cols)]
    for b in range(side):
        up_x[b, mine_x] = up4[b, my_x]
        up_z[b, mine_z] = up4[my_z, b]

    arrived(n_copies)
    for c in reversed(range(CHUNKS)):
        arrived(lambda d: gp_copies(c, d))
    group = side * seq
    gx = gp_x[...].reshape(group, gp_cols)
    gz = gp_z[...].reshape(group, gp_cols)
    for d in (2, 1, 3, 0):
        x, z = lax.rem(my_x + d, side), lax.rem(my_z + d, side)
        first = jnp.dot(n_x[aligned(z, quarter), :], gx, preferred_element_type=F32) * grad_scale
        p_x[z] = first.astype(BF16)
        if d:
            r_copies(d)[1].start()
        for b in range(side):
            at = pl.ds(pl.multiple_of(b * quarter + x * seq, seq), seq)
            second = jnp.dot(n_z[at, :], gz, preferred_element_type=F32) * grad_scale
            p_z[x, b] = second.astype(BF16)
        if d:
            r_copies(d)[0].start()

    arrived(m_copies)
    arrived(up_copies)
    for d in (2, 1, 3, 0):
        x, z = lax.rem(my_x + d, side), lax.rem(my_z + d, side)
        first = jnp.dot(m_x[...], up_x[z], preferred_element_type=F32) * grad_scale
        second = jnp.dot(m_z[...], up_z[x], preferred_element_type=F32) * grad_scale
        o_x[z] = first.astype(BF16)
        o_z[x] = second.astype(BF16)
        if d:
            start(ro_copies(d))

    arrived(r_copies)
    for b in range(side):
        at = slice(b * seq, (b + 1) * seq)
        first = p_x[my_z, at].astype(F32)
        second = p_z[my_x, b].astype(F32)
        for d in (1, 2, 3):
            first = first + r_x[d, at].astype(F32)
            second = second + r_z[d, b].astype(F32)
        s_x[b] = first.astype(BF16)
        s_z[b] = second.astype(BF16)
    for d in (2, 1, 3):
        start(fin_copies(d))
    own_x = pltpu.make_async_copy(s_x.at[my_x], fin_x, own_sem.at[0])
    own_z = pltpu.make_async_copy(s_z.at[my_z], fin_z, own_sem.at[1])
    own_x.start()
    own_z.start()

    arrived(ro_copies)
    first = o_x[my_z].astype(F32)
    second = o_z[my_x].astype(F32)
    for d in (1, 2, 3):
        first = first + ro_x[d].astype(F32)
        second = second + ro_z[d].astype(F32)
    go_buf[:half_in] = first.astype(BF16)
    go_buf[half_in:] = second.astype(BF16)
    go_copy = pltpu.make_async_copy(go_buf, go.at[0], local_sem.at[2 + 2 * CHUNKS])
    go_copy.start()

    for d in (1, 2, 3):
        pairs = [n_copies(d), m_copies(d), up_copies(d), r_copies(d), ro_copies(d)]
        pairs += [gp_copies(c, d) for c in range(CHUNKS)]
        for pair in pairs:
            for copy in pair:
                copy.wait_send()
    for c in range(CHUNKS):

        @pl.when(sec < sections - 1)
        def _():
            for j in range(PIECES):
                fwd_hop(c, j).wait_send()

        @pl.when(sec > 0)
        def _():
            bwd_hop(c).wait_send()

        so_copy(c).wait()
        ig_copy(c).wait()
    go_copy.wait()
    own_x.wait()
    own_z.wait()
    for d in (1, 2, 3):
        for copy in fin_copies(d):
            copy.wait()


def hand_on(*refs):
    count = (len(refs) - 2) // 3
    sems_in, sems_out = refs[-2:]
    loads, stores = [], []
    for i in range(count):
        source, dest, held = refs[i], refs[count + i], refs[2 * count + i]
        rows = source.shape[1] // PARTS
        for j in range(PARTS):
            at, slot = pl.ds(j * rows, rows), i * PARTS + j
            loads.append(pltpu.make_async_copy(source.at[0, at], held.at[at], sems_in.at[slot]))
            stores.append(pltpu.make_async_copy(held.at[at], dest.at[0, at], sems_out.at[slot]))
    for copy in loads:
        copy.start()
    for load, store in zip(loads, stores):
        load.wait()
        store.start()
    for copy in stores:
        copy.wait()


def on_device(tokens_in, cotangent, in_weights, out_weights, slice_lengths):
    seq, width = tokens_in.shape
    inner = out_weights.shape[1]
    heads = inner // HS
    n_dp, side = 16, 4
    group = side * seq
    gp_cols = 3 * inner // 8
    any_space = pl.BlockSpec(memory_space=pl.ANY)
    vmem = pltpu.VMEM
    dma = pltpu.SemaphoreType.DMA
    w_blk = 4
    scratch = [
        vmem((width, 3 * inner), BF16),
        vmem((inner, width), BF16),
        vmem((3 * inner, width), BF16),
        vmem((width, inner), BF16),
        vmem((seq, width), BF16),
        vmem((seq, width), F32),
        vmem((seq, 128), F32),
        vmem((seq, width), BF16),
        vmem((seq, 3 * inner), BF16),
        vmem((heads, seq, seq), F32),
        vmem((seq, inner), BF16),
        vmem((seq, width), BF16),
        vmem((seq, width), BF16),
        vmem((seq, inner), BF16),
        vmem((seq, inner), F32),
        vmem((seq, inner), F32),
        vmem((seq, 3 * inner), BF16),
        vmem((seq, width), F32),
        vmem((seq, width), BF16),
        vmem((width, seq), BF16),
        vmem((inner, seq), BF16),
        vmem((side, side, seq, width // n_dp), BF16),
        vmem((width, group), BF16),
        vmem((width, group), BF16),
        vmem((inner // 2, group), BF16),
        vmem((inner // 2, group), BF16),
        vmem((side, seq, gp_cols), BF16),
        vmem((side, seq, gp_cols), BF16),
        vmem((side, group, width // n_dp), BF16),
        vmem((side, group, width // n_dp), BF16),
        vmem((side, width // side, gp_cols), BF16),
        vmem((side, side, seq, gp_cols), BF16),
        vmem((side, inner // 2, width // n_dp), BF16),
        vmem((side, inner // 2, width // n_dp), BF16),
        vmem((side, width // side, gp_cols), BF16),
        vmem((side, side, seq, gp_cols), BF16),
        vmem((side, seq, gp_cols), BF16),
        vmem((side, seq, gp_cols), BF16),
        vmem((side, inner // 2, width // n_dp), BF16),
        vmem((side, inner // 2, width // n_dp), BF16),
        vmem((inner, width // n_dp), BF16),
        dma((w_blk,)),
        dma,
        dma((3 + 2 * CHUNKS,)),
        dma((2,)),
        dma((CHUNKS, PIECES)),
        dma((CHUNKS, PIECES)),
        dma((CHUNKS,)),
        dma((CHUNKS,)),
        dma((6 + CHUNKS, 2, side)),
        dma((6 + CHUNKS, 2, side)),
    ]
    shapes = (
        jax.ShapeDtypeStruct((1, seq, width), BF16),
        jax.ShapeDtypeStruct((1, seq, width), BF16),
        jax.ShapeDtypeStruct((1, width // n_dp, 3 * inner), BF16),
        jax.ShapeDtypeStruct((1, inner, width // n_dp), BF16),
    )
    results = pl.pallas_call(
        kernel,
        out_shape=shapes,
        in_specs=[pl.BlockSpec(memory_space=pltpu.SMEM)] + [any_space] * 4,
        out_specs=[any_space] * 4,
        scratch_shapes=scratch,
        compiler_params=pltpu.CompilerParams(
            collective_id=0, has_side_effects=True, vmem_limit_bytes=62 << 20
        ),
    )(slice_lengths, tokens_in, cotangent, in_weights, out_weights)
    return pl.pallas_call(
        hand_on,
        out_shape=shapes,
        in_specs=[any_space] * 4,
        out_specs=[any_space] * 4,
        scratch_shapes=[vmem(s.shape[1:], BF16) for s in shapes]
        + [dma((4 * PARTS,)), dma((4 * PARTS,))],
    )(*results)


def solution(mesh):
    placed = (
        P("dp", None),
        P("dp", None),
        P("section", None, None),
        P("section", None, None),
        P("dp", None),
    )
    return jax.shard_map(
        on_device,
        mesh=mesh,
        in_specs=placed,
        out_specs=(
            P("section", "dp", None),
            P("section", "dp", None),
            P("section", "dp", None),
            P("section", None, "dp"),
        ),
        check_vma=False,
    )
```

```python
import math

import jax
import jax.numpy as jnp
from jax import lax
from jax.experimental import pallas as pl
from jax.experimental.pallas import tpu as pltpu
from jax.sharding import PartitionSpec as P

HS = 128
CHUNKS = 2
PIECES = 2
PARTS = 2
SUB = 16
MESH = pl.DeviceIdType.MESH
F32 = jnp.float32
BF16 = jnp.bfloat16


def padded(rows):
    missing = 128 - rows.shape[0]
    if missing <= 0:
        return rows
    return jnp.concatenate([rows, jnp.zeros((missing, rows.shape[1]), rows.dtype)], 0)


def product(rows, weight):
    return jnp.dot(padded(rows), weight, preferred_element_type=F32)[: rows.shape[0]]


def against_rows(left, right):
    return lax.dot_general(left, right, (((1,), (1,)), ((), ())), preferred_element_type=F32)


def over_rows(left, right):
    return lax.dot_general(left, right, (((0,), (0,)), ((), ())), preferred_element_type=F32)


def kernel(
    lens_in,
    tok,
    cot,
    win,
    wout,
    so,
    ig,
    gi,
    go,
    w_in,
    w_out,
    w_in_t,
    w_out_t,
    x_in,
    x_hat,
    inv_std,
    normed,
    proj,
    probs,
    mixed,
    out,
    up,
    grad_mixed,
    key_acc,
    val_acc,
    gp,
    gn,
    gin,
    n_t,
    m_t,
    up4,
    n_x,
    n_z,
    m_x,
    m_z,
    gp_x,
    gp_z,
    up_x,
    up_z,
    p_x,
    p_z,
    o_x,
    o_z,
    r_x,
    r_z,
    s_x,
    s_z,
    ro_x,
    ro_z,
    go_buf,
    lens,
    win_sem,
    wout_sem,
    tok_sem,
    local_sem,
    own_sem,
    fwd_send,
    fwd_recv,
    bwd_send,
    bwd_recv,
    dp_send,
    dp_recv,
):
    sections = 8
    n_dp = 16
    side = 4
    sec = lax.axis_index("section")
    me = lax.axis_index("dp")
    my_z, my_x = me // side, lax.rem(me, side)
    _, seq, width = x_in.shape
    inner = w_out.shape[0]
    heads = inner // HS
    rows_c = seq // CHUNKS
    quarter = width // side
    half_cols = 3 * inner // 2
    gp_cols = half_cols // side
    half_in = inner // 2
    w_blk = win_sem.shape[0]
    scale = 1.0 / math.sqrt(HS)
    grad_scale = 1.0 / math.sqrt(seq * n_dp)
    piece_cols = width // PIECES

    def aligned(index, size):
        return pl.ds(pl.multiple_of(index * size, size), size)

    w_starts = [part * inner + g * half_in for g in (0, 1) for part in range(3)]

    def win_copy(j):
        cols = pl.ds(w_starts[j], half_in)
        return pltpu.make_async_copy(win.at[0, :, cols], w_in.at[:, cols], win_sem.at[j])

    def wout_copy(j):
        cols = pl.ds(j * (width // 2), width // 2)
        return pltpu.make_async_copy(wout.at[0, :, cols], w_out.at[:, cols], wout_sem.at[j])

    def tok_copy(c):
        rows = pl.ds(c * rows_c, rows_c)
        return pltpu.make_async_copy(tok.at[rows], x_in.at[0, rows], tok_sem.at[c])

    lens_copy = pltpu.make_async_copy(lens_in, lens, local_sem.at[0])
    cot_copy = pltpu.make_async_copy(cot, up.at[0], local_sem.at[1])
    in_slot = jnp.where(sec == 0, 0, 1)
    up_slot = jnp.where(sec == sections - 1, 0, 1)

    @pl.when(sec == 0)
    def _():
        for c in range(CHUNKS):
            tok_copy(c).start()

    @pl.when(sec == sections - 1)
    def _():
        cot_copy.start()

    for j in range(w_blk):
        win_copy(j).start()
    for j in (0, 1):
        wout_copy(j).start()
    lens_copy.start()

    def at_x(d):
        return my_z * side + lax.rem(my_x + d, side)

    def at_z(d):
        return lax.rem(my_z + d, side) * side + my_x

    barrier = pltpu.get_barrier_semaphore()
    for d in (1, 2, 3):
        for to in (at_x(d), at_z(d)):
            pl.semaphore_signal(barrier, inc=1, device_id={"dp": to}, device_id_type=MESH)
    for step in (1, sections - 1):
        pl.semaphore_signal(
            barrier,
            inc=1,
            device_id={"section": lax.rem(sec + step, sections)},
            device_id_type=MESH,
        )

    row_at = lax.broadcasted_iota(jnp.int32, (seq, seq), 0)
    col_at = lax.broadcasted_iota(jnp.int32, (seq, seq), 1)
    causal = col_at <= row_at
    if CHUNKS > 1:
        proj[...] = jnp.zeros_like(proj)

    def transpose_weights():
        blk = 512

        def turn(source, dest):
            rows, cols = source.shape
            wide = cols // blk

            def one(i, _):
                r = pl.multiple_of((i // wide) * blk, blk)
                c = pl.multiple_of(lax.rem(i, wide) * blk, blk)
                dest[pl.ds(c, blk), pl.ds(r, blk)] = source[pl.ds(r, blk), pl.ds(c, blk)].T
                return 0

            lax.fori_loop(0, (rows // blk) * wide, one, 0)

        turn(w_in, w_in_t)
        turn(w_out, w_out_t)

    @pl.when(sec > 0)
    def _():
        for j in range(w_blk):
            win_copy(j).wait()
        for j in (0, 1):
            wout_copy(j).wait()

    @pl.when(sec >= sections // 2)
    def _():
        transpose_weights()

    def fwd_hop(c, j):
        at = (pl.ds(c * rows_c, rows_c), pl.ds(j * piece_cols, piece_cols))
        return pltpu.make_async_remote_copy(
            src_ref=out.at[at],
            dst_ref=x_in.at[1].at[at],
            send_sem=fwd_send.at[c, j],
            recv_sem=fwd_recv.at[c, j],
            device_id={"section": lax.rem(sec + 1, sections)},
            device_id_type=MESH,
        )

    def so_copy(c):
        rows = pl.ds(c * rows_c, rows_c)
        return pltpu.make_async_copy(out.at[rows], so.at[0, rows], local_sem.at[2 + c])

    every = list(range(heads))
    q_at = [slice(h * HS, (h + 1) * HS) for h in every]
    k_at = [slice(inner + h * HS, inner + (h + 1) * HS) for h in every]
    v_at = [slice(2 * inner + h * HS, 2 * inner + (h + 1) * HS) for h in every]

    for c in range(CHUNKS):
        r0 = c * rows_c
        rows = slice(r0, r0 + rows_c)

        @pl.when(sec > 0)
        def _():
            for j in range(PIECES):
                fwd_hop(c, j).wait_recv()

        @pl.when(sec == 0)
        def _():
            tok_copy(c).wait()

        for r in range(r0, r0 + rows_c, SUB):
            sub = slice(r, r + SUB)
            values = x_in[in_slot, sub, :].astype(F32)
            centre = jnp.mean(values, -1, keepdims=True)
            shifted = values - centre
            inv = lax.rsqrt(jnp.mean(shifted * shifted, -1, keepdims=True) + 1e-05)
            hat = shifted * inv
            x_hat[sub, :] = hat
            inv_std[sub, :] = jnp.broadcast_to(inv, (SUB, 128))
            normed[sub, :] = hat.astype(BF16)

        def project(blocks, loading):
            for j in blocks:
                if loading:
                    win_copy(j).wait()
                cols = slice(w_starts[j], w_starts[j] + half_in)
                proj[rows, cols] = product(normed[rows, :], w_in[:, cols]).astype(BF16)

        def attend(group):
            seen = causal[rows, :]
            scores = [against_rows(proj[rows, q_at[h]], proj[:, k_at[h]]) for h in group]
            scores = [jnp.where(seen, a, -jnp.inf) for a in scores]
            top = [jnp.max(a, -1, keepdims=True) for a in scores]
            weight = [jnp.exp((a - t) * scale) for a, t in zip(scores, top)]
            total = [1.0 / jnp.sum(a, -1, keepdims=True) for a in weight]
            p = [a * t for a, t in zip(weight, total)]
            for h, a in zip(group, p):
                probs[h, rows, :] = a
            mixes = [
                jnp.dot(a.astype(BF16), proj[:, v_at[h]], preferred_element_type=F32)
                for h, a in zip(group, p)
            ]
            for h, a in zip(group, mixes):
                mixed[rows, q_at[h]] = a.astype(BF16)

        if c == 0:

            @pl.when(sec == 0)
            def _():
                for g in (0, 1):
                    project(range(3 * g, 3 * g + 3), True)
                    attend(every[g * heads // 2 : (g + 1) * heads // 2])
                for j in (0, 1):
                    wout_copy(j).wait()

            @pl.when(sec > 0)
            def _():
                project(range(w_blk), False)
                attend(every)

            pl.semaphore_wait(barrier, 8)
        else:
            project(range(w_blk), False)
            attend(every)

        for j in range(PIECES):
            cols = slice(j * piece_cols, (j + 1) * piece_cols)
            out[rows, cols] = (
                x_in[in_slot, rows, cols].astype(F32) + product(mixed[rows, :], w_out[:, cols])
            ).astype(BF16)
            fwd_hop(c, j).start()

        so_copy(c).start()

    n_kind, m_kind, r_kind, ro_kind, fin_kind, gp_kind = range(6)
    up_kind = gp_kind + CHUNKS
    mine_x, mine_z = aligned(my_x, seq), aligned(my_z, seq)

    def dp_copy(src, dst, kind, axis, d):
        return pltpu.make_async_remote_copy(
            src_ref=src,
            dst_ref=dst,
            send_sem=dp_send.at[kind, axis, d],
            recv_sem=dp_recv.at[kind, axis, d],
            device_id={"dp": at_z(d) if axis else at_x(d)},
            device_id_type=MESH,
        )

    def n_copies(d):
        return (
            dp_copy(n_t, n_x.at[:, mine_x], n_kind, 0, d),
            dp_copy(n_t, n_z.at[:, mine_z], n_kind, 1, d),
        )

    def m_copies(d):
        return (
            dp_copy(m_t.at[:half_in], m_x.at[:, mine_x], m_kind, 0, d),
            dp_copy(m_t.at[half_in:], m_z.at[:, mine_z], m_kind, 1, d),
        )

    def up_copies(c, d):
        x, z = lax.rem(my_x + d, side), lax.rem(my_z + d, side)
        rows = pl.ds(c * rows_c, rows_c)
        to_x = pl.ds(pl.multiple_of(my_x * seq + c * rows_c, rows_c), rows_c)
        to_z = pl.ds(pl.multiple_of(my_z * seq + c * rows_c, rows_c), rows_c)
        return (
            dp_copy(up4.at[:, x, rows], up_x.at[:, to_x], up_kind + c, 0, d),
            dp_copy(up4.at[z, :, rows], up_z.at[:, to_z], up_kind + c, 1, d),
        )

    def gp_copies(c, d):
        x, z = lax.rem(my_x + d, side), lax.rem(my_z + d, side)
        rows = pl.ds(c * rows_c, rows_c)
        z_cols = pl.ds(pl.multiple_of(half_cols + z * gp_cols, gp_cols), gp_cols)
        return (
            dp_copy(
                gp.at[rows, aligned(x, gp_cols)],
                gp_x.at[my_x, rows],
                gp_kind + c,
                0,
                d,
            ),
            dp_copy(gp.at[rows, z_cols], gp_z.at[my_z, rows], gp_kind + c, 1, d),
        )

    def r_copies(d):
        x, z = lax.rem(my_x + d, side), lax.rem(my_z + d, side)
        return (
            dp_copy(p_z.at[x], r_z.at[d], r_kind, 0, d),
            dp_copy(p_x.at[z], r_x.at[d], r_kind, 1, d),
        )

    def ro_copies(d):
        x, z = lax.rem(my_x + d, side), lax.rem(my_z + d, side)
        return (
            dp_copy(o_z.at[x], ro_z.at[d], ro_kind, 0, d),
            dp_copy(o_x.at[z], ro_x.at[d], ro_kind, 1, d),
        )

    fin_x = gi.at[0, :, aligned(my_x, gp_cols)]
    fin_z = gi.at[0, :, pl.ds(pl.multiple_of(half_cols + my_z * gp_cols, gp_cols), gp_cols)]

    def fin_copies(d):
        x, z = lax.rem(my_x + d, side), lax.rem(my_z + d, side)
        return (
            dp_copy(s_x.at[x], fin_x, fin_kind, 0, d),
            dp_copy(s_z.at[z], fin_z, fin_kind, 1, d),
        )

    def start(*pairs):
        for pair in pairs:
            for copy in pair:
                copy.start()

    def arrived(copies):
        for d in (1, 3, 2):
            for copy in copies(d):
                copy.wait_recv()

    def send_forward_operands():
        for r in range(0, width, 512):
            n_t[r : r + 512, :] = normed[:, r : r + 512].T
        for r in range(0, inner, 512):
            m_t[r : r + 512, :] = mixed[:, r : r + 512].T
        for d in (2, 1, 3):
            start(n_copies(d), m_copies(d))
        n_x[:, mine_x] = n_t[...]
        n_z[:, mine_z] = n_t[...]
        m_x[:, mine_x] = m_t[:half_in]
        m_z[:, mine_z] = m_t[half_in:]

    @pl.when(sec < sections - 1)
    def _():
        send_forward_operands()

    @pl.when(sec < sections // 2)
    def _():
        transpose_weights()

    lens_copy.wait()
    row_slice = jnp.zeros((seq, seq), jnp.int32)
    col_slice = jnp.zeros((seq, seq), jnp.int32)
    end = jnp.int32(0)
    for j in range(lens.shape[1]):
        end = end + lens[0, j]
        row_slice = row_slice + jnp.where(row_at >= end, 1, 0)
        col_slice = col_slice + jnp.where(col_at >= end, 1, 0)
    same = row_slice == col_slice

    def bwd_hop(c):
        rows = pl.ds(c * rows_c, rows_c)
        return pltpu.make_async_remote_copy(
            src_ref=gin.at[rows],
            dst_ref=up.at[1].at[rows],
            send_sem=bwd_send.at[c],
            recv_sem=bwd_recv.at[c],
            device_id={"section": lax.rem(sec + sections - 1, sections)},
            device_id_type=MESH,
        )

    def ig_copy(c):
        rows = pl.ds(c * rows_c, rows_c)
        return pltpu.make_async_copy(gin.at[rows], ig.at[0, rows], local_sem.at[2 + CHUNKS + c])

    @pl.when(sec == sections - 1)
    def _():
        cot_copy.wait()

    for c in reversed(range(CHUNKS)):
        r0 = c * rows_c
        rows = slice(r0, r0 + rows_c)

        @pl.when(sec < sections - 1)
        def _():
            bwd_hop(c).wait_recv()

        for j in range(0, inner, 512):
            cols = slice(j, j + 512)
            grad_mixed[rows, cols] = product(up[up_slot, rows, :], w_out_t[:, cols]).astype(BF16)

        live = same[rows, :]
        grad_p = [against_rows(grad_mixed[rows, q_at[h]], proj[:, v_at[h]]) for h in every]
        p = [probs[h, rows, :] for h in every]
        own_p = [jnp.where(live, a, 0.0).astype(BF16) for a in p]
        grad_v = [over_rows(own_p[h], grad_mixed[rows, q_at[h]]) for h in every]
        weighted = [a * b for a, b in zip(p, grad_p)]
        delta = [jnp.sum(a, -1, keepdims=True) for a in weighted]
        grad_s = [a * (b - t) for a, b, t in zip(p, grad_p, delta)]
        grad_q = [
            jnp.dot(grad_s[h].astype(BF16), proj[:, k_at[h]], preferred_element_type=F32)
            for h in every
        ]
        own_s = [jnp.where(live, a, 0.0).astype(BF16) for a in grad_s]
        grad_k = [over_rows(own_s[h], proj[rows, q_at[h]]) for h in every]
        for h in every:
            gk, gv = grad_k[h], grad_v[h]
            if c < CHUNKS - 1:
                gk = gk[: r0 + rows_c] + key_acc[: r0 + rows_c, q_at[h]]
                gv = gv[: r0 + rows_c] + val_acc[: r0 + rows_c, q_at[h]]
            if c > 0:
                key_acc[:r0, q_at[h]] = gk[:r0]
                val_acc[:r0, q_at[h]] = gv[:r0]
            gp[rows, q_at[h]] = (grad_q[h] * scale).astype(BF16)
            gp[rows, k_at[h]] = (gk[rows] * scale).astype(BF16)
            gp[rows, v_at[h]] = gv[rows].astype(BF16)

        for d in (2, 1, 3):
            start(gp_copies(c, d))

        for j in range(0, width, 512):
            cols = slice(j, j + 512)
            gn[rows, cols] = product(gp[rows, :], w_in_t[:, cols])

        for r in range(r0, r0 + rows_c, SUB):
            sub = slice(r, r + SUB)
            g = gn[sub, :]
            hat = x_hat[sub, :]
            mean_g = jnp.mean(g, -1, keepdims=True)
            mean_gh = jnp.mean(g * hat, -1, keepdims=True)
            grad = inv_std[sub, :1] * (g - mean_g - hat * mean_gh)
            gin[sub, :] = (up[up_slot, sub, :].astype(F32) + grad).astype(BF16)

        bwd_hop(c).start()
        ig_copy(c).start()
        for b in range(n_dp):
            up4[b // side, b % side, rows] = up[up_slot, rows, b * seq : (b + 1) * seq]
        for d in (2, 1, 3):
            start(up_copies(c, d))

    @pl.when(sec == sections - 1)
    def _():
        send_forward_operands()

    gp_x[my_x] = gp[:, aligned(my_x, gp_cols)]
    gp_z[my_z] = gp[:, pl.ds(pl.multiple_of(half_cols + my_z * gp_cols, gp_cols), gp_cols)]
    for b in range(side):
        up_x[b, mine_x] = up4[b, my_x]
        up_z[b, mine_z] = up4[my_z, b]

    arrived(n_copies)
    for c in reversed(range(CHUNKS)):
        arrived(lambda d: gp_copies(c, d))
    group = side * seq
    gx = gp_x[...].reshape(group, gp_cols)
    gz = gp_z[...].reshape(group, gp_cols)
    for d in (2, 1, 3, 0):
        x, z = lax.rem(my_x + d, side), lax.rem(my_z + d, side)
        first = jnp.dot(n_x[aligned(z, quarter), :], gx, preferred_element_type=F32) * grad_scale
        p_x[z] = first.astype(BF16)
        if d:
            r_copies(d)[1].start()
        for b in range(side):
            at = pl.ds(pl.multiple_of(b * quarter + x * seq, seq), seq)
            second = jnp.dot(n_z[at, :], gz, preferred_element_type=F32) * grad_scale
            p_z[x, b] = second.astype(BF16)
        if d:
            r_copies(d)[0].start()

    arrived(m_copies)
    for c in reversed(range(CHUNKS)):
        arrived(lambda d: up_copies(c, d))
    for d in (2, 1, 3, 0):
        x, z = lax.rem(my_x + d, side), lax.rem(my_z + d, side)
        first = jnp.dot(m_x[...], up_x[z], preferred_element_type=F32) * grad_scale
        second = jnp.dot(m_z[...], up_z[x], preferred_element_type=F32) * grad_scale
        o_x[z] = first.astype(BF16)
        o_z[x] = second.astype(BF16)
        if d:
            start(ro_copies(d))

    def landed(copies, axis):
        for d in (1, 3, 2):
            copies(d)[axis].wait_recv()

    landed(r_copies, 1)
    for b in range(side):
        at = slice(b * seq, (b + 1) * seq)
        total = p_x[my_z, at].astype(F32)
        for d in (1, 2, 3):
            total = total + r_x[d, at].astype(F32)
        s_x[b] = total.astype(BF16)
    for d in (2, 1, 3):
        fin_copies(d)[0].start()
    landed(r_copies, 0)
    for b in range(side):
        total = p_z[my_x, b].astype(F32)
        for d in (1, 2, 3):
            total = total + r_z[d, b].astype(F32)
        s_z[b] = total.astype(BF16)
    for d in (2, 1, 3):
        fin_copies(d)[1].start()
    own_x = pltpu.make_async_copy(s_x.at[my_x], fin_x, own_sem.at[0])
    own_z = pltpu.make_async_copy(s_z.at[my_z], fin_z, own_sem.at[1])
    own_x.start()
    own_z.start()

    arrived(ro_copies)
    first = o_x[my_z].astype(F32)
    second = o_z[my_x].astype(F32)
    for d in (1, 2, 3):
        first = first + ro_x[d].astype(F32)
        second = second + ro_z[d].astype(F32)
    go_buf[:half_in] = first.astype(BF16)
    go_buf[half_in:] = second.astype(BF16)
    go_copy = pltpu.make_async_copy(go_buf, go.at[0], local_sem.at[2 + 2 * CHUNKS])
    go_copy.start()

    for d in (1, 2, 3):
        pairs = [n_copies(d), m_copies(d), r_copies(d), ro_copies(d)]
        pairs += [gp_copies(c, d) for c in range(CHUNKS)]
        pairs += [up_copies(c, d) for c in range(CHUNKS)]
        for pair in pairs:
            for copy in pair:
                copy.wait_send()
    for c in range(CHUNKS):

        for j in range(PIECES):
            fwd_hop(c, j).wait_send()
        bwd_hop(c).wait_send()

        @pl.when(sec == 0)
        def _():
            for j in range(PIECES):
                fwd_hop(c, j).wait_recv()

        @pl.when(sec == sections - 1)
        def _():
            bwd_hop(c).wait_recv()

        so_copy(c).wait()
        ig_copy(c).wait()
    go_copy.wait()
    own_x.wait()
    own_z.wait()
    for d in (1, 2, 3):
        for copy in fin_copies(d):
            copy.wait()


def hand_on(*refs):
    count = (len(refs) - 2) // 3
    sems_in, sems_out = refs[-2:]
    loads, stores = [], []
    for i in range(count):
        source, dest, held = refs[i], refs[count + i], refs[2 * count + i]
        rows = source.shape[1] // PARTS
        for j in range(PARTS):
            at, slot = pl.ds(j * rows, rows), i * PARTS + j
            loads.append(pltpu.make_async_copy(source.at[0, at], held.at[at], sems_in.at[slot]))
            stores.append(pltpu.make_async_copy(held.at[at], dest.at[0, at], sems_out.at[slot]))
    for copy in loads:
        copy.start()
    for load, store in zip(loads, stores):
        load.wait()
        store.start()
    for copy in stores:
        copy.wait()


def on_device(tokens_in, cotangent, in_weights, out_weights, slice_lengths):
    seq, width = tokens_in.shape
    inner = out_weights.shape[1]
    heads = inner // HS
    n_dp, side = 16, 4
    group = side * seq
    gp_cols = 3 * inner // 8
    any_space = pl.BlockSpec(memory_space=pl.ANY)
    vmem = pltpu.VMEM
    dma = pltpu.SemaphoreType.DMA
    scratch = [
        vmem((width, 3 * inner), BF16),
        vmem((inner, width), BF16),
        vmem((3 * inner, width), BF16),
        vmem((width, inner), BF16),
        vmem((2, seq, width), BF16),
        vmem((seq, width), F32),
        vmem((seq, 128), F32),
        vmem((seq, width), BF16),
        vmem((seq, 3 * inner), BF16),
        vmem((heads, seq, seq), F32),
        vmem((seq, inner), BF16),
        vmem((seq, width), BF16),
        vmem((2, seq, width), BF16),
        vmem((seq, inner), BF16),
        vmem((seq, inner), F32),
        vmem((seq, inner), F32),
        vmem((seq, 3 * inner), BF16),
        vmem((seq, width), F32),
        vmem((seq, width), BF16),
        vmem((width, seq), BF16),
        vmem((inner, seq), BF16),
        vmem((side, side, seq, width // n_dp), BF16),
        vmem((width, group), BF16),
        vmem((width, group), BF16),
        vmem((inner // 2, group), BF16),
        vmem((inner // 2, group), BF16),
        vmem((side, seq, gp_cols), BF16),
        vmem((side, seq, gp_cols), BF16),
        vmem((side, group, width // n_dp), BF16),
        vmem((side, group, width // n_dp), BF16),
        vmem((side, width // side, gp_cols), BF16),
        vmem((side, side, seq, gp_cols), BF16),
        vmem((side, inner // 2, width // n_dp), BF16),
        vmem((side, inner // 2, width // n_dp), BF16),
        vmem((side, width // side, gp_cols), BF16),
        vmem((side, side, seq, gp_cols), BF16),
        vmem((side, seq, gp_cols), BF16),
        vmem((side, seq, gp_cols), BF16),
        vmem((side, inner // 2, width // n_dp), BF16),
        vmem((side, inner // 2, width // n_dp), BF16),
        vmem((inner, width // n_dp), BF16),
        pltpu.SMEM((1, 8), jnp.int32),
        dma((6,)),
        dma((2,)),
        dma((CHUNKS,)),
        dma((3 + 2 * CHUNKS,)),
        dma((2,)),
        dma((CHUNKS, PIECES)),
        dma((CHUNKS, PIECES)),
        dma((CHUNKS,)),
        dma((CHUNKS,)),
        dma((5 + 2 * CHUNKS, 2, side)),
        dma((5 + 2 * CHUNKS, 2, side)),
    ]
    shapes = (
        jax.ShapeDtypeStruct((1, seq, width), BF16),
        jax.ShapeDtypeStruct((1, seq, width), BF16),
        jax.ShapeDtypeStruct((1, width // n_dp, 3 * inner), BF16),
        jax.ShapeDtypeStruct((1, inner, width // n_dp), BF16),
    )
    results = pl.pallas_call(
        kernel,
        out_shape=shapes,
        in_specs=[any_space] * 5,
        out_specs=[any_space] * 4,
        scratch_shapes=scratch,
        compiler_params=pltpu.CompilerParams(
            collective_id=0, has_side_effects=True, vmem_limit_bytes=62 << 20
        ),
    )(slice_lengths, tokens_in, cotangent, in_weights, out_weights)
    return pl.pallas_call(
        hand_on,
        out_shape=shapes,
        in_specs=[any_space] * 4,
        out_specs=[any_space] * 4,
        scratch_shapes=[vmem(s.shape[1:], BF16) for s in shapes]
        + [dma((4 * PARTS,)), dma((4 * PARTS,))],
    )(*results)


def solution(mesh):
    placed = (
        P("dp", None),
        P("dp", None),
        P("section", None, None),
        P("section", None, None),
        P("dp", None),
    )
    return jax.shard_map(
        on_device,
        mesh=mesh,
        in_specs=placed,
        out_specs=(
            P("section", "dp", None),
            P("section", "dp", None),
            P("section", "dp", None),
            P("section", None, "dp"),
        ),
        check_vma=False,
    )
```

```python
import math

import jax
import jax.numpy as jnp
from jax import lax
from jax.experimental import pallas as pl
from jax.experimental.pallas import tpu as pltpu
from jax.sharding import PartitionSpec as P

HS = 128
CHUNKS = 2
PIECES = 2
PARTS = 2
SUB = 16
MESH = pl.DeviceIdType.MESH
F32 = jnp.float32
BF16 = jnp.bfloat16


def padded(rows):
    missing = 128 - rows.shape[0]
    if missing <= 0:
        return rows
    return jnp.concatenate([rows, jnp.zeros((missing, rows.shape[1]), rows.dtype)], 0)


def product(rows, weight):
    return jnp.dot(padded(rows), weight, preferred_element_type=F32)[: rows.shape[0]]


def against_rows(left, right):
    return lax.dot_general(left, right, (((1,), (1,)), ((), ())), preferred_element_type=F32)


def over_rows(left, right):
    return lax.dot_general(left, right, (((0,), (0,)), ((), ())), preferred_element_type=F32)


def kernel(
    lens_in,
    tok,
    cot,
    win,
    wout,
    so,
    ig,
    gi,
    go,
    w_in,
    w_out,
    w_in_t,
    w_out_t,
    x_in,
    x_hat,
    inv_std,
    normed,
    proj,
    probs,
    mixed,
    out,
    up,
    grad_mixed,
    key_acc,
    val_acc,
    gp,
    gn,
    gin,
    n_t,
    m_t,
    up4,
    n_x,
    n_z,
    m_f,
    gp_x,
    gp_z,
    up_f,
    p_x,
    p_z,
    o_g,
    r_x,
    r_z,
    s_x,
    s_z,
    ro_g,
    go_buf,
    lens,
    win_sem,
    wout_sem,
    tok_sem,
    local_sem,
    own_sem,
    fwd_send,
    fwd_recv,
    bwd_send,
    bwd_recv,
    dp_send,
    dp_recv,
):
    sections = 8
    n_dp = 16
    side = 4
    sec = lax.axis_index("section")
    me = lax.axis_index("dp")
    my_z, my_x = me // side, lax.rem(me, side)
    _, seq, width = x_in.shape
    inner = w_out.shape[0]
    heads = inner // HS
    rows_c = seq // CHUNKS
    quarter = width // side
    half_cols = 3 * inner // 2
    gp_cols = half_cols // side
    half_in = inner // 2
    w_blk = win_sem.shape[0]
    scale = 1.0 / math.sqrt(HS)
    grad_scale = 1.0 / math.sqrt(seq * n_dp)
    piece_cols = width // PIECES

    def aligned(index, size):
        return pl.ds(pl.multiple_of(index * size, size), size)

    w_starts = [part * inner + g * half_in for g in (0, 1) for part in range(3)]

    def win_copy(j):
        cols = pl.ds(w_starts[j], half_in)
        return pltpu.make_async_copy(win.at[0, :, cols], w_in.at[:, cols], win_sem.at[j])

    def wout_copy(j):
        cols = pl.ds(j * (width // 2), width // 2)
        return pltpu.make_async_copy(wout.at[0, :, cols], w_out.at[:, cols], wout_sem.at[j])

    def tok_copy(c):
        rows = pl.ds(c * rows_c, rows_c)
        return pltpu.make_async_copy(tok.at[rows], x_in.at[0, rows], tok_sem.at[c])

    lens_copy = pltpu.make_async_copy(lens_in, lens, local_sem.at[0])
    cot_copy = pltpu.make_async_copy(cot, up.at[0], local_sem.at[1])
    in_slot = jnp.where(sec == 0, 0, 1)
    up_slot = jnp.where(sec == sections - 1, 0, 1)

    @pl.when(sec == 0)
    def _():
        for c in range(CHUNKS):
            tok_copy(c).start()

    @pl.when(sec == sections - 1)
    def _():
        cot_copy.start()

    for j in range(w_blk):
        win_copy(j).start()
    for j in (0, 1):
        wout_copy(j).start()
    lens_copy.start()

    def at_x(d):
        return my_z * side + lax.rem(my_x + d, side)

    def at_z(d):
        return lax.rem(my_z + d, side) * side + my_x

    barrier = pltpu.get_barrier_semaphore()
    for d in (1, 2, 3):
        for to in (at_x(d), at_z(d)):
            pl.semaphore_signal(barrier, inc=1, device_id={"dp": to}, device_id_type=MESH)
    for step in (1, sections - 1):
        pl.semaphore_signal(
            barrier,
            inc=1,
            device_id={"section": lax.rem(sec + step, sections)},
            device_id_type=MESH,
        )

    row_at = lax.broadcasted_iota(jnp.int32, (seq, seq), 0)
    col_at = lax.broadcasted_iota(jnp.int32, (seq, seq), 1)
    causal = col_at <= row_at
    if CHUNKS > 1:
        proj[...] = jnp.zeros_like(proj)

    def transpose_weights():
        blk = 512

        def turn(source, dest):
            rows, cols = source.shape
            wide = cols // blk

            def one(i, _):
                r = pl.multiple_of((i // wide) * blk, blk)
                c = pl.multiple_of(lax.rem(i, wide) * blk, blk)
                dest[pl.ds(c, blk), pl.ds(r, blk)] = source[pl.ds(r, blk), pl.ds(c, blk)].T
                return 0

            lax.fori_loop(0, (rows // blk) * wide, one, 0)

        turn(w_in, w_in_t)
        turn(w_out, w_out_t)

    @pl.when(sec > 0)
    def _():
        for j in range(w_blk):
            win_copy(j).wait()
        for j in (0, 1):
            wout_copy(j).wait()

    @pl.when(sec >= sections // 2)
    def _():
        transpose_weights()

    def fwd_hop(c, j):
        at = (pl.ds(c * rows_c, rows_c), pl.ds(j * piece_cols, piece_cols))
        return pltpu.make_async_remote_copy(
            src_ref=out.at[at],
            dst_ref=x_in.at[1].at[at],
            send_sem=fwd_send.at[c, j],
            recv_sem=fwd_recv.at[c, j],
            device_id={"section": lax.rem(sec + 1, sections)},
            device_id_type=MESH,
        )

    def so_copy(c):
        rows = pl.ds(c * rows_c, rows_c)
        return pltpu.make_async_copy(out.at[rows], so.at[0, rows], local_sem.at[2 + c])

    every = list(range(heads))
    q_at = [slice(h * HS, (h + 1) * HS) for h in every]
    k_at = [slice(inner + h * HS, inner + (h + 1) * HS) for h in every]
    v_at = [slice(2 * inner + h * HS, 2 * inner + (h + 1) * HS) for h in every]

    for c in range(CHUNKS):
        r0 = c * rows_c
        rows = slice(r0, r0 + rows_c)

        @pl.when(sec > 0)
        def _():
            for j in range(PIECES):
                fwd_hop(c, j).wait_recv()

        @pl.when(sec == 0)
        def _():
            tok_copy(c).wait()

        for r in range(r0, r0 + rows_c, SUB):
            sub = slice(r, r + SUB)
            values = x_in[in_slot, sub, :].astype(F32)
            centre = jnp.mean(values, -1, keepdims=True)
            shifted = values - centre
            inv = lax.rsqrt(jnp.mean(shifted * shifted, -1, keepdims=True) + 1e-05)
            hat = shifted * inv
            x_hat[sub, :] = hat
            inv_std[sub, :] = jnp.broadcast_to(inv, (SUB, 128))
            normed[sub, :] = hat.astype(BF16)

        def project(blocks, loading):
            for j in blocks:
                if loading:
                    win_copy(j).wait()
                cols = slice(w_starts[j], w_starts[j] + half_in)
                proj[rows, cols] = product(normed[rows, :], w_in[:, cols]).astype(BF16)

        def attend(group):
            seen = causal[rows, :]
            scores = [against_rows(proj[rows, q_at[h]], proj[:, k_at[h]]) for h in group]
            scores = [jnp.where(seen, a, -jnp.inf) for a in scores]
            top = [jnp.max(a, -1, keepdims=True) for a in scores]
            weight = [jnp.exp((a - t) * scale) for a, t in zip(scores, top)]
            total = [1.0 / jnp.sum(a, -1, keepdims=True) for a in weight]
            p = [a * t for a, t in zip(weight, total)]
            for h, a in zip(group, p):
                probs[h, rows, :] = a
            mixes = [
                jnp.dot(a.astype(BF16), proj[:, v_at[h]], preferred_element_type=F32)
                for h, a in zip(group, p)
            ]
            for h, a in zip(group, mixes):
                mixed[rows, q_at[h]] = a.astype(BF16)

        if c == 0:

            @pl.when(sec == 0)
            def _():
                for g in (0, 1):
                    project(range(3 * g, 3 * g + 3), True)
                    attend(every[g * heads // 2 : (g + 1) * heads // 2])
                for j in (0, 1):
                    wout_copy(j).wait()

            @pl.when(sec > 0)
            def _():
                project(range(w_blk), False)
                attend(every)

            pl.semaphore_wait(barrier, 8)
        else:
            project(range(w_blk), False)
            attend(every)

        for j in range(PIECES):
            cols = slice(j * piece_cols, (j + 1) * piece_cols)
            out[rows, cols] = (
                x_in[in_slot, rows, cols].astype(F32) + product(mixed[rows, :], w_out[:, cols])
            ).astype(BF16)
            fwd_hop(c, j).start()

        so_copy(c).start()

    n_kind, m_kind, r_kind, ro_kind, fin_kind, gp_kind = range(6)
    up_kind = gp_kind + CHUNKS
    late_r_kind = up_kind + CHUNKS
    mine_x, mine_z = aligned(my_x, seq), aligned(my_z, seq)

    def dp_copy(src, dst, kind, axis, d):
        return pltpu.make_async_remote_copy(
            src_ref=src,
            dst_ref=dst,
            send_sem=dp_send.at[kind, axis, d],
            recv_sem=dp_recv.at[kind, axis, d],
            device_id={"dp": at_z(d) if axis else at_x(d)},
            device_id_type=MESH,
        )

    def n_copies(d):
        return (
            dp_copy(n_t, n_x.at[:, mine_x], n_kind, 0, d),
            dp_copy(n_t, n_z.at[:, mine_z], n_kind, 1, d),
        )

    odd = lax.rem(sec, 2) == 1
    my_f = jnp.where(odd, my_z, my_x)
    my_g = jnp.where(odd, my_x, my_z)
    mine_f = aligned(my_f, seq)

    def one_copy(src, dst, kind, second, d):
        return pltpu.make_async_remote_copy(
            src_ref=src,
            dst_ref=dst,
            send_sem=dp_send.at[kind, 0, d],
            recv_sem=dp_recv.at[kind, 0, d],
            device_id={"dp": jnp.where(odd != second, at_z(d), at_x(d))},
            device_id_type=MESH,
        )

    def m_copies(d):
        return (one_copy(m_t, m_f.at[:, mine_f], m_kind, False, d),)

    def up_copies(c, d):
        rows = pl.ds(c * rows_c, rows_c)
        to = pl.ds(pl.multiple_of(my_f * seq + c * rows_c, rows_c), rows_c)
        src = up4.at[lax.rem(my_f + d, side), :, rows]
        return (one_copy(src, up_f.at[:, to], up_kind + c, False, d),)

    def gp_copies(c, d):
        x, z = lax.rem(my_x + d, side), lax.rem(my_z + d, side)
        rows = pl.ds(c * rows_c, rows_c)
        z_cols = pl.ds(pl.multiple_of(half_cols + z * gp_cols, gp_cols), gp_cols)
        return (
            dp_copy(
                gp.at[rows, aligned(x, gp_cols)],
                gp_x.at[my_x, rows],
                gp_kind + c,
                0,
                d,
            ),
            dp_copy(gp.at[rows, z_cols], gp_z.at[my_z, rows], gp_kind + c, 1, d),
        )

    order = (2, 1, 3, 0)

    def r_copies(half, d):
        x, z = lax.rem(my_x + d, side), lax.rem(my_z + d, side)
        kind = late_r_kind if half else r_kind
        blocks = pl.ds(2 * half, 2)
        return (
            dp_copy(p_z.at[x, blocks], r_z.at[d, blocks], kind, 0, d),
            dp_copy(p_x.at[z, blocks], r_x.at[d, blocks], kind, 1, d),
        )

    def ro_copies(d):
        return (one_copy(o_g.at[lax.rem(my_g + d, side)], ro_g.at[d], ro_kind, True, d),)

    fin_x = gi.at[0, :, aligned(my_x, gp_cols)]
    fin_z = gi.at[0, :, pl.ds(pl.multiple_of(half_cols + my_z * gp_cols, gp_cols), gp_cols)]

    def fin_copies(d):
        return (
            dp_copy(s_x.at[d], fin_x, fin_kind, 0, d),
            dp_copy(s_z.at[d], fin_z, fin_kind, 1, d),
        )

    def start(*pairs):
        for pair in pairs:
            for copy in pair:
                copy.start()

    def arrived(copies):
        for d in (1, 3, 2):
            for copy in copies(d):
                copy.wait_recv()

    def send_forward_operands():
        for r in range(0, width, 512):
            n_t[r : r + 512, :] = normed[:, r : r + 512].T
        for r in range(0, inner, 512):
            m_t[r : r + 512, :] = mixed[:, r : r + 512].T
        for d in (2, 1, 3):
            start(n_copies(d), m_copies(d))
        n_x[:, mine_x] = n_t[...]
        n_z[:, mine_z] = n_t[...]
        m_f[:, mine_f] = m_t[...]

    @pl.when(sec < sections - 1)
    def _():
        send_forward_operands()

    @pl.when(sec < sections // 2)
    def _():
        transpose_weights()

    lens_copy.wait()
    row_slice = jnp.zeros((seq, seq), jnp.int32)
    col_slice = jnp.zeros((seq, seq), jnp.int32)
    end = jnp.int32(0)
    for j in range(lens.shape[1]):
        end = end + lens[0, j]
        row_slice = row_slice + jnp.where(row_at >= end, 1, 0)
        col_slice = col_slice + jnp.where(col_at >= end, 1, 0)
    same = row_slice == col_slice

    def bwd_hop(c):
        rows = pl.ds(c * rows_c, rows_c)
        return pltpu.make_async_remote_copy(
            src_ref=gin.at[rows],
            dst_ref=up.at[1].at[rows],
            send_sem=bwd_send.at[c],
            recv_sem=bwd_recv.at[c],
            device_id={"section": lax.rem(sec + sections - 1, sections)},
            device_id_type=MESH,
        )

    def ig_copy(c):
        rows = pl.ds(c * rows_c, rows_c)
        return pltpu.make_async_copy(gin.at[rows], ig.at[0, rows], local_sem.at[2 + CHUNKS + c])

    @pl.when(sec == sections - 1)
    def _():
        cot_copy.wait()

    for c in reversed(range(CHUNKS)):
        r0 = c * rows_c
        rows = slice(r0, r0 + rows_c)

        @pl.when(sec < sections - 1)
        def _():
            bwd_hop(c).wait_recv()

        for j in range(0, inner, 512):
            cols = slice(j, j + 512)
            grad_mixed[rows, cols] = product(up[up_slot, rows, :], w_out_t[:, cols]).astype(BF16)

        live = same[rows, :]
        grad_p = [against_rows(grad_mixed[rows, q_at[h]], proj[:, v_at[h]]) for h in every]
        p = [probs[h, rows, :] for h in every]
        own_p = [jnp.where(live, a, 0.0).astype(BF16) for a in p]
        grad_v = [over_rows(own_p[h], grad_mixed[rows, q_at[h]]) for h in every]
        weighted = [a * b for a, b in zip(p, grad_p)]
        delta = [jnp.sum(a, -1, keepdims=True) for a in weighted]
        grad_s = [a * (b - t) for a, b, t in zip(p, grad_p, delta)]
        grad_q = [
            jnp.dot(grad_s[h].astype(BF16), proj[:, k_at[h]], preferred_element_type=F32)
            for h in every
        ]
        own_s = [jnp.where(live, a, 0.0).astype(BF16) for a in grad_s]
        grad_k = [over_rows(own_s[h], proj[rows, q_at[h]]) for h in every]
        for h in every:
            gk, gv = grad_k[h], grad_v[h]
            if c < CHUNKS - 1:
                gk = gk[: r0 + rows_c] + key_acc[: r0 + rows_c, q_at[h]]
                gv = gv[: r0 + rows_c] + val_acc[: r0 + rows_c, q_at[h]]
            if c > 0:
                key_acc[:r0, q_at[h]] = gk[:r0]
                val_acc[:r0, q_at[h]] = gv[:r0]
            gp[rows, q_at[h]] = (grad_q[h] * scale).astype(BF16)
            gp[rows, k_at[h]] = (gk[rows] * scale).astype(BF16)
            gp[rows, v_at[h]] = gv[rows].astype(BF16)

        for d in (2, 1, 3):
            start(gp_copies(c, d))

        for j in range(0, width, 512):
            cols = slice(j, j + 512)
            gn[rows, cols] = product(gp[rows, :], w_in_t[:, cols])

        for r in range(r0, r0 + rows_c, SUB):
            sub = slice(r, r + SUB)
            g = gn[sub, :]
            hat = x_hat[sub, :]
            mean_g = jnp.mean(g, -1, keepdims=True)
            mean_gh = jnp.mean(g * hat, -1, keepdims=True)
            grad = inv_std[sub, :1] * (g - mean_g - hat * mean_gh)
            gin[sub, :] = (up[up_slot, sub, :].astype(F32) + grad).astype(BF16)

        bwd_hop(c).start()
        ig_copy(c).start()
        for b in range(n_dp):
            f = jnp.where(odd, b // side, b % side)
            g = jnp.where(odd, b % side, b // side)
            up4[f, g, rows] = up[up_slot, rows, b * seq : (b + 1) * seq]
        for d in (2, 1, 3):
            start(up_copies(c, d))

    @pl.when(sec == sections - 1)
    def _():
        send_forward_operands()

    gp_x[my_x] = gp[:, aligned(my_x, gp_cols)]
    gp_z[my_z] = gp[:, pl.ds(pl.multiple_of(half_cols + my_z * gp_cols, gp_cols), gp_cols)]
    for b in range(side):
        up_f[b, mine_f] = up4[my_f, b]

    arrived(n_copies)
    for c in reversed(range(CHUNKS)):
        arrived(lambda d: gp_copies(c, d))
    group = side * seq
    gx = gp_x[...].reshape(group, gp_cols)
    gz = gp_z[...].reshape(group, gp_cols)
    for half in (0, 1):
        for d in order:
            x, z = lax.rem(my_x + d, side), lax.rem(my_z + d, side)
            for place in (2 * half, 2 * half + 1):
                to_x = lax.rem(my_x + order[place], side)
                to_z = lax.rem(my_z + order[place], side)
                at_first = pl.ds(pl.multiple_of(z * quarter + to_x * seq, seq), seq)
                first = jnp.dot(n_x[at_first, :], gx, preferred_element_type=F32)
                p_x[z, place] = (first * grad_scale).astype(BF16)
                at_second = pl.ds(pl.multiple_of(to_z * quarter + x * seq, seq), seq)
                second = jnp.dot(n_z[at_second, :], gz, preferred_element_type=F32)
                p_z[x, place] = (second * grad_scale).astype(BF16)
            if d:
                start(r_copies(half, d))

    arrived(m_copies)
    for c in reversed(range(CHUNKS)):
        arrived(lambda d: up_copies(c, d))
    for d in (2, 1, 3, 0):
        g = lax.rem(my_g + d, side)
        total = jnp.dot(m_f[...], up_f[g], preferred_element_type=F32) * grad_scale
        o_g[g] = total.astype(BF16)
        if d:
            start(ro_copies(d))

    def landed(copies, axis):
        for d in (1, 3, 2):
            copies(d)[axis].wait_recv()

    for half in (0, 1):
        for axis in (1, 0):
            landed(lambda d: r_copies(half, d), axis)
            own, arrivals, sums = (p_x, r_x, s_x) if axis else (p_z, r_z, s_z)
            for place in (2 * half, 2 * half + 1):
                total = own[my_z if axis else my_x, place].astype(F32)
                for d in (1, 2, 3):
                    total = total + arrivals[d, place].astype(F32)
                sums[order[place]] = total.astype(BF16)
                if order[place]:
                    fin_copies(order[place])[1 - axis].start()
    own_x = pltpu.make_async_copy(s_x.at[0], fin_x, own_sem.at[0])
    own_z = pltpu.make_async_copy(s_z.at[0], fin_z, own_sem.at[1])
    own_x.start()
    own_z.start()

    arrived(ro_copies)
    total = o_g[my_g].astype(F32)
    for d in (1, 2, 3):
        total = total + ro_g[d].astype(F32)
    go_buf[...] = total.astype(BF16)
    go_copy = pltpu.make_async_copy(go_buf, go.at[0], local_sem.at[2 + 2 * CHUNKS])
    go_copy.start()

    for d in (1, 2, 3):
        pairs = [n_copies(d), m_copies(d), r_copies(0, d), r_copies(1, d), ro_copies(d)]
        pairs += [gp_copies(c, d) for c in range(CHUNKS)]
        pairs += [up_copies(c, d) for c in range(CHUNKS)]
        for pair in pairs:
            for copy in pair:
                copy.wait_send()
    for c in range(CHUNKS):

        for j in range(PIECES):
            fwd_hop(c, j).wait_send()
        bwd_hop(c).wait_send()

        @pl.when(sec == 0)
        def _():
            for j in range(PIECES):
                fwd_hop(c, j).wait_recv()

        @pl.when(sec == sections - 1)
        def _():
            bwd_hop(c).wait_recv()

        so_copy(c).wait()
        ig_copy(c).wait()
    go_copy.wait()
    own_x.wait()
    own_z.wait()
    for d in (1, 2, 3):
        for copy in fin_copies(d):
            copy.wait()


def hand_on(*refs):
    count = (len(refs) - 2) // 3
    sems_in, sems_out = refs[-2:]
    loads, stores = [], []
    for i in range(count):
        source, dest, held = refs[i], refs[count + i], refs[2 * count + i]
        rows = source.shape[1] // PARTS
        for j in range(PARTS):
            at, slot = pl.ds(j * rows, rows), i * PARTS + j
            loads.append(pltpu.make_async_copy(source.at[0, at], held.at[at], sems_in.at[slot]))
            stores.append(pltpu.make_async_copy(held.at[at], dest.at[0, at], sems_out.at[slot]))
    for copy in loads:
        copy.start()
    for load, store in zip(loads, stores):
        load.wait()
        store.start()
    for copy in stores:
        copy.wait()


def on_device(tokens_in, cotangent, in_weights, out_weights, slice_lengths):
    seq, width = tokens_in.shape
    inner = out_weights.shape[1]
    heads = inner // HS
    n_dp, side = 16, 4
    group = side * seq
    gp_cols = 3 * inner // 8
    any_space = pl.BlockSpec(memory_space=pl.ANY)
    vmem = pltpu.VMEM
    dma = pltpu.SemaphoreType.DMA
    scratch = [
        vmem((width, 3 * inner), BF16),
        vmem((inner, width), BF16),
        vmem((3 * inner, width), BF16),
        vmem((width, inner), BF16),
        vmem((2, seq, width), BF16),
        vmem((seq, width), F32),
        vmem((seq, 128), F32),
        vmem((seq, width), BF16),
        vmem((seq, 3 * inner), BF16),
        vmem((heads, seq, seq), F32),
        vmem((seq, inner), BF16),
        vmem((seq, width), BF16),
        vmem((2, seq, width), BF16),
        vmem((seq, inner), BF16),
        vmem((seq, inner), F32),
        vmem((seq, inner), F32),
        vmem((seq, 3 * inner), BF16),
        vmem((seq, width), F32),
        vmem((seq, width), BF16),
        vmem((width, seq), BF16),
        vmem((inner, seq), BF16),
        vmem((side, side, seq, width // n_dp), BF16),
        vmem((width, group), BF16),
        vmem((width, group), BF16),
        vmem((inner, group), BF16),
        vmem((side, seq, gp_cols), BF16),
        vmem((side, seq, gp_cols), BF16),
        vmem((side, group, width // n_dp), BF16),
        vmem((side, side, seq, gp_cols), BF16),
        vmem((side, side, seq, gp_cols), BF16),
        vmem((side, inner, width // n_dp), BF16),
        vmem((side, side, seq, gp_cols), BF16),
        vmem((side, side, seq, gp_cols), BF16),
        vmem((side, seq, gp_cols), BF16),
        vmem((side, seq, gp_cols), BF16),
        vmem((side, inner, width // n_dp), BF16),
        vmem((inner, width // n_dp), BF16),
        pltpu.SMEM((1, 8), jnp.int32),
        dma((6,)),
        dma((2,)),
        dma((CHUNKS,)),
        dma((3 + 2 * CHUNKS,)),
        dma((2,)),
        dma((CHUNKS, PIECES)),
        dma((CHUNKS, PIECES)),
        dma((CHUNKS,)),
        dma((CHUNKS,)),
        dma((6 + 2 * CHUNKS, 2, side)),
        dma((6 + 2 * CHUNKS, 2, side)),
    ]
    shapes = (
        jax.ShapeDtypeStruct((1, seq, width), BF16),
        jax.ShapeDtypeStruct((1, seq, width), BF16),
        jax.ShapeDtypeStruct((1, width // n_dp, 3 * inner), BF16),
        jax.ShapeDtypeStruct((1, inner, width // n_dp), BF16),
    )
    results = pl.pallas_call(
        kernel,
        out_shape=shapes,
        in_specs=[any_space] * 5,
        out_specs=[any_space] * 4,
        scratch_shapes=scratch,
        compiler_params=pltpu.CompilerParams(
            collective_id=0, has_side_effects=True, vmem_limit_bytes=62 << 20
        ),
    )(slice_lengths, tokens_in, cotangent, in_weights, out_weights)
    return pl.pallas_call(
        hand_on,
        out_shape=shapes,
        in_specs=[any_space] * 4,
        out_specs=[any_space] * 4,
        scratch_shapes=[vmem(s.shape[1:], BF16) for s in shapes]
        + [dma((4 * PARTS,)), dma((4 * PARTS,))],
    )(*results)


def solution(mesh):
    placed = (
        P("dp", None),
        P("dp", None),
        P("section", None, None),
        P("section", None, None),
        P("dp", None),
    )
    return jax.shard_map(
        on_device,
        mesh=mesh,
        in_specs=placed,
        out_specs=(
            P("section", "dp", None),
            P("section", "dp", None),
            P("section", "dp", None),
            P("section", None, "dp"),
        ),
        check_vma=False,
    )
```

```python
import math

import jax
import jax.numpy as jnp
from jax import lax
from jax.experimental import pallas as pl
from jax.experimental.pallas import tpu as pltpu
from jax.sharding import PartitionSpec as P

HS = 128
CHUNKS = 2
PIECES = 2
PARTS = 2
SUB = 16
MESH = pl.DeviceIdType.MESH
F32 = jnp.float32
BF16 = jnp.bfloat16


def padded(rows):
    missing = 128 - rows.shape[0]
    if missing <= 0:
        return rows
    return jnp.concatenate([rows, jnp.zeros((missing, rows.shape[1]), rows.dtype)], 0)


def product(rows, weight):
    return jnp.dot(padded(rows), weight, preferred_element_type=F32)[: rows.shape[0]]


def against_rows(left, right):
    return lax.dot_general(left, right, (((1,), (1,)), ((), ())), preferred_element_type=F32)


def over_rows(left, right):
    return lax.dot_general(left, right, (((0,), (0,)), ((), ())), preferred_element_type=F32)


def kernel(
    lens_in,
    tok,
    cot,
    win,
    wout,
    so,
    ig,
    gi,
    go,
    w_in,
    w_out,
    w_in_t,
    w_out_t,
    x_in,
    x_hat,
    inv_std,
    normed,
    proj,
    probs,
    mixed,
    out,
    up,
    grad_mixed,
    key_acc,
    val_acc,
    gp,
    gn,
    gin,
    n_t,
    m_t,
    up4,
    n_x,
    n_z,
    m_f,
    gp_x,
    gp_z,
    up_f,
    p_x,
    p_z,
    o_g,
    r_x,
    r_z,
    s_x,
    s_z,
    ro_g,
    go_buf,
    lens,
    win_sem,
    wout_sem,
    tok_sem,
    local_sem,
    own_sem,
    fwd_send,
    fwd_recv,
    bwd_send,
    bwd_recv,
    dp_send,
    dp_recv,
):
    sections = 8
    n_dp = 16
    side = 4
    sec = lax.axis_index("section")
    me = lax.axis_index("dp")
    my_z, my_x = me // side, lax.rem(me, side)
    _, seq, width = x_in.shape
    inner = w_out.shape[0]
    heads = inner // HS
    rows_c = seq // CHUNKS
    quarter = width // side
    half_cols = 3 * inner // 2
    gp_cols = half_cols // side
    half_in = inner // 2
    w_blk = win_sem.shape[0]
    scale = 1.0 / math.sqrt(HS)
    grad_scale = 1.0 / math.sqrt(seq * n_dp)
    piece_cols = width // PIECES

    def aligned(index, size):
        return pl.ds(pl.multiple_of(index * size, size), size)

    w_starts = [part * inner + g * half_in for g in (0, 1) for part in range(3)]

    def win_copy(j):
        cols = pl.ds(w_starts[j], half_in)
        return pltpu.make_async_copy(win.at[0, :, cols], w_in.at[:, cols], win_sem.at[j])

    def wout_copy(j):
        cols = pl.ds(j * (width // 2), width // 2)
        return pltpu.make_async_copy(wout.at[0, :, cols], w_out.at[:, cols], wout_sem.at[j])

    def tok_copy(c):
        rows = pl.ds(c * rows_c, rows_c)
        return pltpu.make_async_copy(tok.at[rows], x_in.at[0, rows], tok_sem.at[c])

    lens_copy = pltpu.make_async_copy(lens_in, lens, local_sem.at[0])
    cot_copy = pltpu.make_async_copy(cot, up.at[0], local_sem.at[1])
    in_slot = jnp.where(sec == 0, 0, 1)
    up_slot = jnp.where(sec == sections - 1, 0, 1)

    @pl.when(sec == 0)
    def _():
        for c in range(CHUNKS):
            tok_copy(c).start()

    @pl.when(sec == sections - 1)
    def _():
        cot_copy.start()

    for j in range(w_blk):
        win_copy(j).start()
    for j in (0, 1):
        wout_copy(j).start()
    lens_copy.start()

    def at_x(d):
        return my_z * side + lax.rem(my_x + d, side)

    def at_z(d):
        return lax.rem(my_z + d, side) * side + my_x

    barrier = pltpu.get_barrier_semaphore()
    for d in (1, 2, 3):
        for to in (at_x(d), at_z(d)):
            pl.semaphore_signal(barrier, inc=1, device_id={"dp": to}, device_id_type=MESH)
    for step in (1, sections - 1):
        pl.semaphore_signal(
            barrier,
            inc=1,
            device_id={"section": lax.rem(sec + step, sections)},
            device_id_type=MESH,
        )

    row_at = lax.broadcasted_iota(jnp.int32, (seq, seq), 0)
    col_at = lax.broadcasted_iota(jnp.int32, (seq, seq), 1)
    causal = col_at <= row_at
    if CHUNKS > 1:
        proj[...] = jnp.zeros_like(proj)

    def transpose_weights():
        blk = 512

        def turn(source, dest):
            rows, cols = source.shape
            wide = cols // blk

            def one(i, _):
                r = pl.multiple_of((i // wide) * blk, blk)
                c = pl.multiple_of(lax.rem(i, wide) * blk, blk)
                dest[pl.ds(c, blk), pl.ds(r, blk)] = source[pl.ds(r, blk), pl.ds(c, blk)].T
                return 0

            lax.fori_loop(0, (rows // blk) * wide, one, 0)

        turn(w_in, w_in_t)
        turn(w_out, w_out_t)

    @pl.when(sec > 0)
    def _():
        for j in range(w_blk):
            win_copy(j).wait()
        for j in (0, 1):
            wout_copy(j).wait()

    @pl.when(sec >= sections // 2)
    def _():
        transpose_weights()

    def fwd_hop(c, j):
        at = (pl.ds(c * rows_c, rows_c), pl.ds(j * piece_cols, piece_cols))
        return pltpu.make_async_remote_copy(
            src_ref=out.at[at],
            dst_ref=x_in.at[1].at[at],
            send_sem=fwd_send.at[c, j],
            recv_sem=fwd_recv.at[c, j],
            device_id={"section": lax.rem(sec + 1, sections)},
            device_id_type=MESH,
        )

    def so_copy(c):
        rows = pl.ds(c * rows_c, rows_c)
        return pltpu.make_async_copy(out.at[rows], so.at[0, rows], local_sem.at[2 + c])

    every = list(range(heads))
    q_at = [slice(h * HS, (h + 1) * HS) for h in every]
    k_at = [slice(inner + h * HS, inner + (h + 1) * HS) for h in every]
    v_at = [slice(2 * inner + h * HS, 2 * inner + (h + 1) * HS) for h in every]

    for c in range(CHUNKS):
        r0 = c * rows_c
        rows = slice(r0, r0 + rows_c)

        @pl.when(sec > 0)
        def _():
            for j in range(PIECES):
                fwd_hop(c, j).wait_recv()

        @pl.when(sec == 0)
        def _():
            tok_copy(c).wait()

        for r in range(r0, r0 + rows_c, SUB):
            sub = slice(r, r + SUB)
            values = x_in[in_slot, sub, :].astype(F32)
            centre = jnp.mean(values, -1, keepdims=True)
            shifted = values - centre
            inv = lax.rsqrt(jnp.mean(shifted * shifted, -1, keepdims=True) + 1e-05)
            hat = shifted * inv
            x_hat[sub, :] = hat
            inv_std[sub, :] = jnp.broadcast_to(inv, (SUB, 128))
            normed[sub, :] = hat.astype(BF16)

        def project(blocks, loading):
            for j in blocks:
                if loading:
                    win_copy(j).wait()
                cols = slice(w_starts[j], w_starts[j] + half_in)
                proj[rows, cols] = product(normed[rows, :], w_in[:, cols]).astype(BF16)

        def attend(group):
            seen = causal[rows, :]
            scores = [against_rows(proj[rows, q_at[h]], proj[:, k_at[h]]) for h in group]
            scores = [jnp.where(seen, a, -jnp.inf) for a in scores]
            top = [jnp.max(a, -1, keepdims=True) for a in scores]
            weight = [jnp.exp((a - t) * scale) for a, t in zip(scores, top)]
            total = [1.0 / jnp.sum(a, -1, keepdims=True) for a in weight]
            p = [a * t for a, t in zip(weight, total)]
            for h, a in zip(group, p):
                probs[h, rows, :] = a
            mixes = [
                jnp.dot(a.astype(BF16), proj[:, v_at[h]], preferred_element_type=F32)
                for h, a in zip(group, p)
            ]
            for h, a in zip(group, mixes):
                mixed[rows, q_at[h]] = a.astype(BF16)

        if c == 0:

            @pl.when(sec == 0)
            def _():
                for g in (0, 1):
                    project(range(3 * g, 3 * g + 3), True)
                    attend(every[g * heads // 2 : (g + 1) * heads // 2])
                for j in (0, 1):
                    wout_copy(j).wait()

            @pl.when(sec > 0)
            def _():
                project(range(w_blk), False)
                attend(every)

            pl.semaphore_wait(barrier, 8)
        else:
            project(range(w_blk), False)
            attend(every)

        for j in range(PIECES):
            cols = slice(j * piece_cols, (j + 1) * piece_cols)
            out[rows, cols] = (
                x_in[in_slot, rows, cols].astype(F32) + product(mixed[rows, :], w_out[:, cols])
            ).astype(BF16)
            fwd_hop(c, j).start()

        so_copy(c).start()

    n_kind, m_kind, r_kind, ro_kind, fin_kind, gp_kind = range(6)
    up_kind = gp_kind + CHUNKS
    late_r_kind = up_kind + CHUNKS
    mine_x, mine_z = aligned(my_x, seq), aligned(my_z, seq)

    def dp_copy(src, dst, kind, axis, d):
        return pltpu.make_async_remote_copy(
            src_ref=src,
            dst_ref=dst,
            send_sem=dp_send.at[kind, axis, d],
            recv_sem=dp_recv.at[kind, axis, d],
            device_id={"dp": at_z(d) if axis else at_x(d)},
            device_id_type=MESH,
        )

    def n_copies(d):
        return (
            dp_copy(n_t, n_x.at[:, mine_x], n_kind, 0, d),
            dp_copy(n_t, n_z.at[:, mine_z], n_kind, 1, d),
        )

    odd = lax.rem(sec, 2) == 1
    my_f = jnp.where(odd, my_z, my_x)
    my_g = jnp.where(odd, my_x, my_z)
    mine_f = aligned(my_f, seq)

    def one_copy(src, dst, kind, second, d):
        return pltpu.make_async_remote_copy(
            src_ref=src,
            dst_ref=dst,
            send_sem=dp_send.at[kind, 0, d],
            recv_sem=dp_recv.at[kind, 0, d],
            device_id={"dp": jnp.where(odd != second, at_z(d), at_x(d))},
            device_id_type=MESH,
        )

    def m_copies(d):
        return (one_copy(m_t, m_f.at[:, mine_f], m_kind, False, d),)

    def up_copies(c, d):
        rows = pl.ds(c * rows_c, rows_c)
        to = pl.ds(pl.multiple_of(my_f * seq + c * rows_c, rows_c), rows_c)
        src = up4.at[lax.rem(my_f + d, side), :, rows]
        return (one_copy(src, up_f.at[:, to], up_kind + c, False, d),)

    def gp_copies(c, d):
        x, z = lax.rem(my_x + d, side), lax.rem(my_z + d, side)
        rows = pl.ds(c * rows_c, rows_c)
        z_cols = pl.ds(pl.multiple_of(half_cols + z * gp_cols, gp_cols), gp_cols)
        return (
            dp_copy(
                gp.at[rows, aligned(x, gp_cols)],
                gp_x.at[my_x, rows],
                gp_kind + c,
                0,
                d,
            ),
            dp_copy(gp.at[rows, z_cols], gp_z.at[my_z, rows], gp_kind + c, 1, d),
        )

    order = (1, 3, 2, 0)

    def r_copies(half, d):
        x, z = lax.rem(my_x + d, side), lax.rem(my_z + d, side)
        kind = late_r_kind if half else r_kind
        blocks = pl.ds(2 * half, 2)
        return (
            dp_copy(p_z.at[x, blocks], r_z.at[d, blocks], kind, 0, d),
            dp_copy(p_x.at[z, blocks], r_x.at[d, blocks], kind, 1, d),
        )

    def ro_copies(d):
        return (one_copy(o_g.at[lax.rem(my_g + d, side)], ro_g.at[d], ro_kind, True, d),)

    fin_x = gi.at[0, :, aligned(my_x, gp_cols)]
    fin_z = gi.at[0, :, pl.ds(pl.multiple_of(half_cols + my_z * gp_cols, gp_cols), gp_cols)]

    def fin_copies(d):
        return (
            dp_copy(s_x.at[d], fin_x, fin_kind, 0, d),
            dp_copy(s_z.at[d], fin_z, fin_kind, 1, d),
        )

    def start(*pairs):
        for pair in pairs:
            for copy in pair:
                copy.start()

    def arrived(copies):
        for d in (1, 3, 2):
            for copy in copies(d):
                copy.wait_recv()

    def send_forward_operands():
        for r in range(0, width, 512):
            n_t[r : r + 512, :] = normed[:, r : r + 512].T
        for r in range(0, inner, 512):
            m_t[r : r + 512, :] = mixed[:, r : r + 512].T
        for d in (2, 1, 3):
            start(n_copies(d), m_copies(d))
        n_x[:, mine_x] = n_t[...]
        n_z[:, mine_z] = n_t[...]
        m_f[:, mine_f] = m_t[...]

    @pl.when(sec < sections - 1)
    def _():
        send_forward_operands()

    @pl.when(sec < sections // 2)
    def _():
        transpose_weights()

    lens_copy.wait()
    row_slice = jnp.zeros((seq, seq), jnp.int32)
    col_slice = jnp.zeros((seq, seq), jnp.int32)
    end = jnp.int32(0)
    for j in range(lens.shape[1]):
        end = end + lens[0, j]
        row_slice = row_slice + jnp.where(row_at >= end, 1, 0)
        col_slice = col_slice + jnp.where(col_at >= end, 1, 0)
    same = row_slice == col_slice

    def bwd_hop(c):
        rows = pl.ds(c * rows_c, rows_c)
        return pltpu.make_async_remote_copy(
            src_ref=gin.at[rows],
            dst_ref=up.at[1].at[rows],
            send_sem=bwd_send.at[c],
            recv_sem=bwd_recv.at[c],
            device_id={"section": lax.rem(sec + sections - 1, sections)},
            device_id_type=MESH,
        )

    def ig_copy(c):
        rows = pl.ds(c * rows_c, rows_c)
        return pltpu.make_async_copy(gin.at[rows], ig.at[0, rows], local_sem.at[2 + CHUNKS + c])

    @pl.when(sec == sections - 1)
    def _():
        cot_copy.wait()

    for c in reversed(range(CHUNKS)):
        r0 = c * rows_c
        rows = slice(r0, r0 + rows_c)

        @pl.when(sec < sections - 1)
        def _():
            bwd_hop(c).wait_recv()

        for j in range(0, inner, 512):
            cols = slice(j, j + 512)
            grad_mixed[rows, cols] = product(up[up_slot, rows, :], w_out_t[:, cols]).astype(BF16)

        live = same[rows, :]
        grad_p = [against_rows(grad_mixed[rows, q_at[h]], proj[:, v_at[h]]) for h in every]
        p = [probs[h, rows, :] for h in every]
        own_p = [jnp.where(live, a, 0.0).astype(BF16) for a in p]
        grad_v = [over_rows(own_p[h], grad_mixed[rows, q_at[h]]) for h in every]
        weighted = [a * b for a, b in zip(p, grad_p)]
        delta = [jnp.sum(a, -1, keepdims=True) for a in weighted]
        grad_s = [a * (b - t) for a, b, t in zip(p, grad_p, delta)]
        grad_q = [
            jnp.dot(grad_s[h].astype(BF16), proj[:, k_at[h]], preferred_element_type=F32)
            for h in every
        ]
        own_s = [jnp.where(live, a, 0.0).astype(BF16) for a in grad_s]
        grad_k = [over_rows(own_s[h], proj[rows, q_at[h]]) for h in every]
        for h in every:
            gk, gv = grad_k[h], grad_v[h]
            if c < CHUNKS - 1:
                gk = gk[: r0 + rows_c] + key_acc[: r0 + rows_c, q_at[h]]
                gv = gv[: r0 + rows_c] + val_acc[: r0 + rows_c, q_at[h]]
            if c > 0:
                key_acc[:r0, q_at[h]] = gk[:r0]
                val_acc[:r0, q_at[h]] = gv[:r0]
            gp[rows, q_at[h]] = (grad_q[h] * scale).astype(BF16)
            gp[rows, k_at[h]] = (gk[rows] * scale).astype(BF16)
            gp[rows, v_at[h]] = gv[rows].astype(BF16)

        for d in (2, 1, 3):
            start(gp_copies(c, d))

        for j in range(0, width, 512):
            cols = slice(j, j + 512)
            gn[rows, cols] = product(gp[rows, :], w_in_t[:, cols])

        for r in range(r0, r0 + rows_c, SUB):
            sub = slice(r, r + SUB)
            g = gn[sub, :]
            hat = x_hat[sub, :]
            mean_g = jnp.mean(g, -1, keepdims=True)
            mean_gh = jnp.mean(g * hat, -1, keepdims=True)
            grad = inv_std[sub, :1] * (g - mean_g - hat * mean_gh)
            gin[sub, :] = (up[up_slot, sub, :].astype(F32) + grad).astype(BF16)

        bwd_hop(c).start()
        ig_copy(c).start()
        for b in range(n_dp):
            f = jnp.where(odd, b // side, b % side)
            g = jnp.where(odd, b % side, b // side)
            up4[f, g, rows] = up[up_slot, rows, b * seq : (b + 1) * seq]
        for d in (2, 1, 3):
            start(up_copies(c, d))

    @pl.when(sec == sections - 1)
    def _():
        send_forward_operands()

    gp_x[my_x] = gp[:, aligned(my_x, gp_cols)]
    gp_z[my_z] = gp[:, pl.ds(pl.multiple_of(half_cols + my_z * gp_cols, gp_cols), gp_cols)]
    for b in range(side):
        up_f[b, mine_f] = up4[my_f, b]

    arrived(n_copies)
    for c in reversed(range(CHUNKS)):
        arrived(lambda d: gp_copies(c, d))
    group = side * seq
    gx = gp_x[...].reshape(group, gp_cols)
    gz = gp_z[...].reshape(group, gp_cols)
    for half in (0, 1):
        for d in order:
            x, z = lax.rem(my_x + d, side), lax.rem(my_z + d, side)
            for place in (2 * half, 2 * half + 1):
                to_x = lax.rem(my_x + order[place], side)
                to_z = lax.rem(my_z + order[place], side)
                at_first = pl.ds(pl.multiple_of(z * quarter + to_x * seq, seq), seq)
                first = jnp.dot(n_x[at_first, :], gx, preferred_element_type=F32)
                p_x[z, place] = (first * grad_scale).astype(BF16)
                at_second = pl.ds(pl.multiple_of(to_z * quarter + x * seq, seq), seq)
                second = jnp.dot(n_z[at_second, :], gz, preferred_element_type=F32)
                p_z[x, place] = (second * grad_scale).astype(BF16)
            if d:
                start(r_copies(half, d))

    arrived(m_copies)
    for c in reversed(range(CHUNKS)):
        arrived(lambda d: up_copies(c, d))
    for d in (2, 1, 3, 0):
        g = lax.rem(my_g + d, side)
        total = jnp.dot(m_f[...], up_f[g], preferred_element_type=F32) * grad_scale
        o_g[g] = total.astype(BF16)
        if d:
            start(ro_copies(d))

    def landed(copies, axis):
        for d in (1, 3, 2):
            copies(d)[axis].wait_recv()

    for half in (0, 1):
        for axis in (1, 0):
            landed(lambda d: r_copies(half, d), axis)
            own, arrivals, sums = (p_x, r_x, s_x) if axis else (p_z, r_z, s_z)
            for place in (2 * half, 2 * half + 1):
                total = own[my_z if axis else my_x, place].astype(F32)
                for d in (1, 2, 3):
                    total = total + arrivals[d, place].astype(F32)
                sums[order[place]] = total.astype(BF16)
                if order[place]:
                    fin_copies(order[place])[1 - axis].start()
    own_x = pltpu.make_async_copy(s_x.at[0], fin_x, own_sem.at[0])
    own_z = pltpu.make_async_copy(s_z.at[0], fin_z, own_sem.at[1])
    own_x.start()
    own_z.start()

    arrived(ro_copies)
    total = o_g[my_g].astype(F32)
    for d in (1, 2, 3):
        total = total + ro_g[d].astype(F32)
    go_buf[...] = total.astype(BF16)
    go_copy = pltpu.make_async_copy(go_buf, go.at[0], local_sem.at[2 + 2 * CHUNKS])
    go_copy.start()

    for d in (1, 2, 3):
        pairs = [n_copies(d), m_copies(d), r_copies(0, d), r_copies(1, d), ro_copies(d)]
        pairs += [gp_copies(c, d) for c in range(CHUNKS)]
        pairs += [up_copies(c, d) for c in range(CHUNKS)]
        for pair in pairs:
            for copy in pair:
                copy.wait_send()
    for c in range(CHUNKS):

        for j in range(PIECES):
            fwd_hop(c, j).wait_send()
        bwd_hop(c).wait_send()

        @pl.when(sec == 0)
        def _():
            for j in range(PIECES):
                fwd_hop(c, j).wait_recv()

        @pl.when(sec == sections - 1)
        def _():
            bwd_hop(c).wait_recv()

        so_copy(c).wait()
        ig_copy(c).wait()
    go_copy.wait()
    own_x.wait()
    own_z.wait()
    for d in (1, 2, 3):
        for copy in fin_copies(d):
            copy.wait()


def hand_on(*refs):
    count = (len(refs) - 2) // 3
    sems_in, sems_out = refs[-2:]
    loads, stores = [], []
    for i in range(count):
        source, dest, held = refs[i], refs[count + i], refs[2 * count + i]
        rows = source.shape[1] // PARTS
        for j in range(PARTS):
            at, slot = pl.ds(j * rows, rows), i * PARTS + j
            loads.append(pltpu.make_async_copy(source.at[0, at], held.at[at], sems_in.at[slot]))
            stores.append(pltpu.make_async_copy(held.at[at], dest.at[0, at], sems_out.at[slot]))
    for copy in loads:
        copy.start()
    for load, store in zip(loads, stores):
        load.wait()
        store.start()
    for copy in stores:
        copy.wait()


def on_device(tokens_in, cotangent, in_weights, out_weights, slice_lengths):
    seq, width = tokens_in.shape
    inner = out_weights.shape[1]
    heads = inner // HS
    n_dp, side = 16, 4
    group = side * seq
    gp_cols = 3 * inner // 8
    any_space = pl.BlockSpec(memory_space=pl.ANY)
    vmem = pltpu.VMEM
    dma = pltpu.SemaphoreType.DMA
    scratch = [
        vmem((width, 3 * inner), BF16),
        vmem((inner, width), BF16),
        vmem((3 * inner, width), BF16),
        vmem((width, inner), BF16),
        vmem((2, seq, width), BF16),
        vmem((seq, width), F32),
        vmem((seq, 128), F32),
        vmem((seq, width), BF16),
        vmem((seq, 3 * inner), BF16),
        vmem((heads, seq, seq), F32),
        vmem((seq, inner), BF16),
        vmem((seq, width), BF16),
        vmem((2, seq, width), BF16),
        vmem((seq, inner), BF16),
        vmem((seq, inner), F32),
        vmem((seq, inner), F32),
        vmem((seq, 3 * inner), BF16),
        vmem((seq, width), F32),
        vmem((seq, width), BF16),
        vmem((width, seq), BF16),
        vmem((inner, seq), BF16),
        vmem((side, side, seq, width // n_dp), BF16),
        vmem((width, group), BF16),
        vmem((width, group), BF16),
        vmem((inner, group), BF16),
        vmem((side, seq, gp_cols), BF16),
        vmem((side, seq, gp_cols), BF16),
        vmem((side, group, width // n_dp), BF16),
        vmem((side, side, seq, gp_cols), BF16),
        vmem((side, side, seq, gp_cols), BF16),
        vmem((side, inner, width // n_dp), BF16),
        vmem((side, side, seq, gp_cols), BF16),
        vmem((side, side, seq, gp_cols), BF16),
        vmem((side, seq, gp_cols), BF16),
        vmem((side, seq, gp_cols), BF16),
        vmem((side, inner, width // n_dp), BF16),
        vmem((inner, width // n_dp), BF16),
        pltpu.SMEM((1, 8), jnp.int32),
        dma((6,)),
        dma((2,)),
        dma((CHUNKS,)),
        dma((3 + 2 * CHUNKS,)),
        dma((2,)),
        dma((CHUNKS, PIECES)),
        dma((CHUNKS, PIECES)),
        dma((CHUNKS,)),
        dma((CHUNKS,)),
        dma((6 + 2 * CHUNKS, 2, side)),
        dma((6 + 2 * CHUNKS, 2, side)),
    ]
    shapes = (
        jax.ShapeDtypeStruct((1, seq, width), BF16),
        jax.ShapeDtypeStruct((1, seq, width), BF16),
        jax.ShapeDtypeStruct((1, width // n_dp, 3 * inner), BF16),
        jax.ShapeDtypeStruct((1, inner, width // n_dp), BF16),
    )
    results = pl.pallas_call(
        kernel,
        out_shape=shapes,
        in_specs=[any_space] * 5,
        out_specs=[any_space] * 4,
        scratch_shapes=scratch,
        compiler_params=pltpu.CompilerParams(
            collective_id=0, has_side_effects=True, vmem_limit_bytes=62 << 20
        ),
    )(slice_lengths, tokens_in, cotangent, in_weights, out_weights)
    return pl.pallas_call(
        hand_on,
        out_shape=shapes,
        in_specs=[any_space] * 4,
        out_specs=[any_space] * 4,
        scratch_shapes=[vmem(s.shape[1:], BF16) for s in shapes]
        + [dma((4 * PARTS,)), dma((4 * PARTS,))],
    )(*results)


def solution(mesh):
    placed = (
        P("dp", None),
        P("dp", None),
        P("section", None, None),
        P("section", None, None),
        P("dp", None),
    )
    return jax.shard_map(
        on_device,
        mesh=mesh,
        in_specs=placed,
        out_specs=(
            P("section", "dp", None),
            P("section", "dp", None),
            P("section", "dp", None),
            P("section", None, "dp"),
        ),
        check_vma=False,
    )
```
